32 devices in a mesh: section: 4 (over z), dp: 8 (over y, x, core).
Axes of the slice: x: 2, y: 2, z: 4, core: 2. Of those that a mesh axis runs over, the one named last changes fastest.
Arguments:
- block_input: bfloat16 [16, 512, 768], P('dp'), may hold values from -6 to 6
- out_cotangent: bfloat16 [16, 512, 768], P('dp'), may hold values from -6 to 6
- lengths: int32 [16], P('dp'), may hold values from 128 to 512, as said below
- ln_gain: float32 [4, 768], P('section'), may hold values from 0.5 to 1.5
- ln_bias: float32 [4, 768], P('section'), may hold values from -0.5 to 0.5
- w_in: bfloat16 [4, 768, 1536], P('section'), may hold values from -0.21875 to 0.21875
- b_in: bfloat16 [4, 1536], P('section'), may hold values from -3 to 3
- w_out: bfloat16 [4, 1536, 768], P('section'), may hold values from -0.109375 to 0.109375
- b_out: bfloat16 [4, 384], P('section'), may hold values from -3 to 3
Outputs:
- section_outputs: bfloat16 [4, 16, 512, 768], P('section', 'dp')
- input_grads: float32 [4, 16, 512, 768], P('section', 'dp')
- ln_gain_grad: float32 [4, 768], P('section')
- ln_bias_grad: float32 [4, 768], P('section')
- w_in_grad: float32 [4, 768, 1536], P('section')
- b_in_grad: float32 [4, 1536], P('section')
- w_out_grad: float32 [4, 1536, 768], P('section')
- b_out_grad: float32 [4, 384], P('section')
The draws below stay inside these ranges and needn't reach their ends.
Inputs may be any that keep to these rules, and one draw needn't show every extreme that they name: `lengths`: each row uses at least a quarter of its slots, and in every draw some row uses all 512.
All inputs are finite; a program needn't handle non-finite values.
Results may differ from the reference program's by a relative error of at most 0.015.
Values may be sent and summed in bfloat16 or wider, within the bound.
A program may use at most 128 MiB of HBM per device.

```python
import math
import jax
import jax.numpy as jnp
from jax import lax

D = 768
FF = 3072
SEQ = 512
ROWS = 16
N_SECTION = 4


def draw_lengths(key, part):
    key = jax.random.fold_in(key, 7)
    first_key, second_key = jax.random.split(key)
    base = jax.random.randint(first_key, (ROWS,), SEQ // 4, SEQ + 1, dtype=jnp.int32)
    chosen = jax.random.randint(second_key, (), 0, ROWS, dtype=jnp.int32)
    return base.at[chosen].set(SEQ)


def levels(rng, extent, pieces, smallest, high):
    def one(position, shards_of):
        steps = jax.random.uniform(jax.random.fold_in(jax.random.fold_in(rng, 6), position), (shards_of,), jnp.float32, smallest / len(pieces), high / len(pieces))
        return jnp.repeat(jnp.exp(steps), extent[position] // shards_of).reshape((-1,) + (1,) * (len(extent) - position - 1))

    loudness = one(*pieces[0])
    for cut in pieces[1:]:
        loudness = loudness * one(*cut)
    return loudness


def bell_draw(stream_key, dims, scale, bound, cuts=(), kind=jnp.bfloat16):
    factor_of = levels(stream_key, dims, cuts, -0.22, 0.18) if cuts else 1.0
    array = jax.random.normal(stream_key, dims, jnp.float32) * scale * factor_of
    return jnp.minimum(jnp.maximum(array, -bound), bound).astype(kind)


def setup_inputs(seed: int = 0) -> dict:
    key_of = jax.random.split(jax.random.key(seed), 10)
    block_input = bell_draw(key_of[0], (ROWS, SEQ, D), 1.0, 6.0, ((0, 8),))
    out_cotangent = bell_draw(key_of[1], (ROWS, SEQ, D), 1.0, 6.0, ((0, 8),))
    lengths = draw_lengths(jax.random.fold_in(key_of[9], 71), 0)
    ln_gain = jnp.clip(1.0 + 0.1 * jax.random.normal(key_of[3], (N_SECTION, D), jnp.float32), 0.5, 1.5)
    ln_bias = jnp.clip(jax.random.uniform(key_of[4], (N_SECTION, D), jnp.float32, -0.5, 0.5) * levels(key_of[4], (N_SECTION, D), ((0, 4),), -0.4, 0.0), -0.5, 0.5)
    w_in = bell_draw(key_of[5], (N_SECTION, D, FF // 2), D ** -0.5, 0.21875, ((0, 4),))
    b_in = bell_draw(key_of[6], (N_SECTION, FF // 2), 0.5, 3.0, ((0, 4),))
    w_out = bell_draw(key_of[7], (N_SECTION, FF // 2, D), FF ** -0.5, 0.109375, ((0, 4),))
    b_out = bell_draw(key_of[8], (N_SECTION, D // 2), 0.5, 3.0, ((0, 4),))
    return {"block_input": block_input, "out_cotangent": out_cotangent, "lengths": lengths, "ln_gain": ln_gain, "ln_bias": ln_bias, "w_in": w_in, "b_in": b_in, "w_out": w_out, "b_out": b_out}


HIGH = lax.Precision.HIGHEST
EPS = 1e-05

@jax.custom_vjp
def low(v):
    return lax.optimization_barrier(v.astype(jnp.bfloat16)).astype(jnp.float32)

@jax.custom_vjp
def low_back(v):
    return v

def low_keep(v):
    return (low(v), None)

def low_pass(kept, grad):
    return (grad,)

def back_keep(v):
    return (v, None)

def back_low(kept, grad):
    return (low(grad),)
low.defvjp(low_keep, low_pass)
low_back.defvjp(back_keep, back_low)

def dft_pair(length):
    positions = jnp.arange(length, dtype=jnp.int32)
    turns = positions[:, None] * positions[None, :] % length
    angle = turns.astype(jnp.float32) * (2.0 * math.pi / length)
    scale = 1.0 / math.sqrt(length)
    return (jnp.cos(angle) * scale, jnp.sin(angle) * scale)

def rounded_table(table):
    return lax.optimization_barrier(table.astype(jnp.bfloat16)).astype(jnp.float32)

def make_tables():
    cos_width, sin_width = dft_pair(D)
    cos_seq, sin_seq = dft_pair(SEQ)
    width_table = rounded_table(jnp.concatenate([cos_width, sin_width], axis=1))
    seq_table = rounded_table(jnp.concatenate([cos_seq, -sin_seq], axis=1))
    return (width_table, seq_table)

def exact_gelu(values):
    return jax.nn.gelu(values, approximate=False)

def layer_norm(summed, norm_gain, norm_bias):
    centre = summed - lax.optimization_barrier(jnp.mean(summed, axis=-1, keepdims=True))
    spread = lax.optimization_barrier(jnp.mean(centre * centre, axis=-1, keepdims=True))
    return centre * lax.rsqrt(spread + EPS) * norm_gain + norm_bias

def mixing_section(hidden, masks, norm_gain, norm_bias, width_table, seq_table):
    spectral = low_back(low(jnp.einsum('gsd,de->gse', hidden, width_table, precision=HIGH)))
    stacked = jnp.concatenate([spectral[..., :D], spectral[..., D:]], axis=1)
    mixed = low_back(jnp.einsum('st,gtd->gsd', seq_table, stacked, precision=HIGH))
    return low(layer_norm(hidden + mixed, norm_gain, norm_bias) * masks)

def forward_section(hidden, masks, norm_gain, norm_bias, w_first, bias_first, w_second, bias_second):
    pre = low_back(jnp.einsum('gsd,df->gsf', hidden, w_first, precision=HIGH) + bias_first)
    active = low_back(low(exact_gelu(pre)))
    branch = low_back(jnp.einsum('gsf,fd->gsd', active, w_second, precision=HIGH) + bias_second)
    return low(layer_norm(hidden + branch, norm_gain, norm_bias) * masks)

def forward(inputs, probes, masks, ln_gain, ln_bias, w_in, b_in, w_out, b_out, width_table, seq_table):
    hidden = inputs * masks + probes[0]
    produced = []
    for which in range(N_SECTION):
        if which % 2 == 0:
            result = mixing_section(hidden, masks, ln_gain[which], ln_bias[which], width_table, seq_table)
        else:
            w_first = jnp.concatenate([w_in[which - 1], w_in[which]], axis=1)
            bias_first = jnp.concatenate([b_in[which - 1], b_in[which]])
            w_second = jnp.concatenate([w_out[which - 1], w_out[which]], axis=0)
            bias_second = jnp.concatenate([b_out[which - 1], b_out[which]])
            result = forward_section(hidden, masks, ln_gain[which], ln_bias[which], w_first, bias_first, w_second, bias_second)
        produced.append(result)
        if which + 1 < N_SECTION:
            hidden = low_back(result) + probes[which + 1]
    return jnp.stack(produced)

def reference(block_input, out_cotangent, lengths, ln_gain, ln_bias, w_in, b_in, w_out, b_out):
    width_table, seq_table = make_tables()
    group = math.gcd(ROWS, 8)
    blocks = ROWS // group
    params = (ln_gain.astype(jnp.float32), ln_bias.astype(jnp.float32), w_in.astype(jnp.float32), b_in.astype(jnp.float32), w_out.astype(jnp.float32), b_out.astype(jnp.float32))
    inputs_all = block_input.astype(jnp.float32).reshape(blocks, group, SEQ, D)
    cotangents_all = out_cotangent.astype(jnp.float32).reshape(blocks, group, SEQ, D)
    lengths_all = lengths.reshape(blocks, group)

    def one_group(totals, group_item):
        inputs, row_cotangents, row_lengths = group_item
        positions = jnp.arange(SEQ, dtype=jnp.int32)
        masks = (positions[None, :] < row_lengths[:, None]).astype(jnp.float32)[..., None]
        probes = jnp.zeros((N_SECTION, group, SEQ, D), jnp.float32)

        def run(probe_values, gains, biases, first_w, first_b, second_w, second_b):
            return forward(inputs, probe_values, masks, gains, biases, first_w, first_b, second_w, second_b, width_table, seq_table)
        produced, pullback = jax.vjp(run, probes, *params)
        full_cotangent = jnp.zeros_like(produced).at[N_SECTION - 1].set(row_cotangents)
        grads = pullback(full_cotangent)
        totals = tuple((old + new for old, new in zip(totals, grads[1:])))
        return (totals, (produced.astype(jnp.bfloat16), grads[0]))
    init = tuple((jnp.zeros_like(value) for value in params))
    totals, (acts, probe_grads) = lax.scan(one_group, init, (inputs_all, cotangents_all, lengths_all))
    acts = jnp.transpose(acts, (1, 0, 2, 3, 4)).reshape(N_SECTION, ROWS, SEQ, D)
    probe_grads = jnp.transpose(probe_grads, (1, 0, 2, 3, 4)).reshape(N_SECTION, ROWS, SEQ, D)
    return (acts, probe_grads, totals[0], totals[1], totals[2], totals[3], totals[4], totals[5])
```

```python
import functools
import math

import jax
import jax.numpy as jnp
import ml_dtypes
import numpy as np
from jax import lax
from jax.experimental import pallas as pl
from jax.experimental.pallas import tpu as pltpu
from jax.sharding import PartitionSpec as P

MESH = pl.DeviceIdType.MESH
F32, BF16 = jnp.float32, jnp.bfloat16
EPS = 1e-05
CHUNK = 128
ROOT_HALF = 1.0 / math.sqrt(2.0)
PDF_SCALE = 1.0 / math.sqrt(2.0 * math.pi)


def dft_pair(length):
    positions = np.arange(length, dtype=np.int64)
    angle = (positions[:, None] * positions[None, :] % length) * (2.0 * math.pi / length)
    scale = 1.0 / math.sqrt(length)
    return np.cos(angle) * scale, np.sin(angle) * scale


def dot(a, b):
    return jnp.dot(a, b, preferred_element_type=F32)


def dot_cols(a, b):
    return lax.dot_general(a, b, (((1,), (1,)), ((), ())), preferred_element_type=F32)


def dot_rows(a, b):
    return lax.dot_general(a, b, (((0,), (0,)), ((), ())), preferred_element_type=F32)


def gelu_pair(v):
    cdf = 0.5 * (1.0 + lax.erf(v * ROOT_HALF))
    return v * cdf, cdf + v * (jnp.exp(-0.5 * v * v) * PDF_SCALE)


def normalize(z):
    centre = z - jnp.mean(z, axis=-1, keepdims=True)
    spread = jnp.mean(centre * centre, axis=-1, keepdims=True)
    inverse = lax.rsqrt(spread + EPS)
    return centre * inverse, inverse


def norm_back(dy, normed, inverse, gain):
    e = dy * gain
    return inverse * (
        e - jnp.mean(e, axis=-1, keepdims=True) - normed * jnp.mean(e * normed, axis=-1, keepdims=True)
    )


def remote(src, dst, send, recv, device):
    return pltpu.make_async_remote_copy(
        src_ref=src, dst_ref=dst, send_sem=send, recv_sem=recv, device_id=device, device_id_type=MESH
    )


def relay(
    dp_count,
    lengths, x_hbm, cot_hbm, gain_ref, bias_ref, b_in_ref, b_out_ref, w1_hbm, w2_hbm, wt_hbm, st_hbm,
    so_hbm, ig_hbm, gw_hbm, small_ref,
    w1, w2, w1x, w2x, wt, st, hin, gin, rxa, rxb, h1, hout, dzb, gout, gmix, act, gp, actx, gpx, sp, dm,
    zacc, nrm, inv, msk, par, G, RC, R1, R2, sms, smr, smv,
    s_load, s_out, par_s, par_r, h_s, h_r, g_s, g_r, pa_s, pa_r, pb_s, pb_r,
    wz_s, wz_r, wf_s, wf_r, wc_s, wc_r, rc_s, rc_r, r1_s, r1_r, r2_s, r2_r, ag_s, ag_r, oc_s, oc_r, sm_s, sm_r,
):
    section = lax.axis_index("section")
    d = lax.axis_index("dp")
    core = lax.rem(d, 2)
    parity = lax.rem(section, 2)
    n_rows, seq, width = hin.shape
    half = w1.shape[1]
    chunks = seq // CHUNK
    tiles = half // 512
    levels = int(math.log2(dp_count)) - 1
    bits = [2 << k for k in range(levels)]

    def flipped(bit):
        return d + bit - 2 * bit * lax.rem(d // bit, 2)

    def by_core(first, second):
        return first + core * (second - first)

    bit_value = [lax.rem(d // b, 2) for b in bits]
    value = [by_core(bit_value[k], bit_value[levels - 1 - k]) for k in range(levels)]
    peer = [(section, by_core(flipped(bits[k]), flipped(bits[levels - 1 - k]))) for k in range(levels)]
    twin = (section, d + 1 - 2 * core)
    pair = (section + 1 - 2 * parity, d)
    up = (section + 1, d)
    down = (section - 1, d)

    def rows_of(t):
        return pl.ds(t * CHUNK, CHUNK)

    load_x = pltpu.make_async_copy(x_hbm, hin, s_load.at[0])
    load_cot = pltpu.make_async_copy(cot_hbm, gin, s_load.at[1])
    load_wt = pltpu.make_async_copy(wt_hbm, wt, s_load.at[2])
    load_st = pltpu.make_async_copy(st_hbm, st, s_load.at[3])
    load_w1 = pltpu.make_async_copy(w1_hbm, w1, s_load.at[4])
    load_w2 = pltpu.make_async_copy(w2_hbm, w2, s_load.at[5])

    @pl.when(section < 2)
    def _():
        load_x.start()
        load_wt.start()
        load_st.start()
        load_w1.start()
        load_w2.start()

    @pl.when(section >= 2)
    def _():
        load_w1.start()
        load_w2.start()
        load_wt.start()
        load_st.start()
        load_cot.start()

    par[parity] = jnp.zeros(par.shape[1:], F32)
    par[parity, 0:1, 0:width] = gain_ref[...]
    par[parity, 1:2, 0:width] = bias_ref[...]
    par[parity, 2:3, :] = b_in_ref[...].astype(F32)
    par[parity, 3:4, pl.ds(pl.multiple_of(parity * (width // 2), 128), width // 2)] = b_out_ref[...].astype(F32)
    smv[...] = jnp.zeros(smv.shape, F32)
    for r in range(n_rows):
        position = lax.broadcasted_iota(jnp.int32, (seq, 1), 0)
        msk[r] = jnp.where(position < lengths[r], 1.0, 0.0).astype(F32)

    barrier = pltpu.get_barrier_semaphore()

    def greet(device):
        pl.semaphore_signal(barrier, inc=1, device_id=device, device_id_type=MESH)

    greet(twin)
    for k in range(levels):
        greet(peer[k])
    pl.when(section > 0)(lambda: greet(down))
    pl.when(section < 3)(lambda: greet(up))
    pl.semaphore_wait(barrier, 1 + levels + jnp.where((section == 0) | (section == 3), 1, 2))

    swap_par = remote(par.at[parity], par.at[parity], par_s, par_r, pair)
    swap_par.start()

    quarter = half // 4
    chip = lax.rem(d // 2, 4)
    chip_far = 3 - chip
    chip_a = chip + 1 - 2 * lax.rem(chip, 2)
    chip_b = 3 - chip_a

    def part1(q):
        return pl.ds(pl.multiple_of(q * quarter, 128), quarter)

    def swap(which, q, src, send, recv, device):
        if which == 0:
            ref, to = (w1 if src == "own" else w1x), w1x
            return remote(ref.at[:, part1(q)], to.at[:, part1(q)], send, recv, device)
        ref, to = (w2 if src == "own" else w2x), w2x
        return remote(ref.at[part1(q)], to.at[part1(q)], send, recv, device)

    near_a = (section, flipped(2))
    near_b = (section, flipped(4))

    def each_core(fn):
        for which in range(2):
            pl.when(core == which)(functools.partial(fn, which))

    def weights_begin():
        load_w1.wait()
        load_w2.wait()

        def go(which):
            swap(which, chip, "own", wz_s.at[0], wz_r.at[0], pair).start()
            swap(which, chip_far, "own", wz_s.at[1], wz_r.at[1], pair).start()

        each_core(go)

    def weights_spread():
        def go(which):
            swap(which, chip, "own", wz_s.at[0], wz_r.at[0], pair).wait_recv()
            swap(which, chip, "got", wf_s.at[0], wf_r.at[0], near_a).start()
            swap(which, chip, "got", wf_s.at[1], wf_r.at[1], near_b).start()
            swap(which, chip, "got", wc_s.at[0], wc_r.at[0], twin).start()

        each_core(go)

    def weights_end():
        def go(which):
            swap(which, chip_a, "got", wf_s.at[0], wf_r.at[0], near_a).wait_recv()
            swap(which, chip_a, "got", wc_s.at[1], wc_r.at[1], twin).start()
            swap(which, chip_b, "got", wf_s.at[1], wf_r.at[1], near_b).wait_recv()
            swap(which, chip_b, "got", wc_s.at[2], wc_r.at[2], twin).start()
            swap(which, chip_far, "own", wz_s.at[1], wz_r.at[1], pair).wait_recv()
            swap(which, chip_far, "got", wc_s.at[3], wc_r.at[3], twin).start()
            other = 1 - which
            for i, q in enumerate((chip, chip_a, chip_b, chip_far)):
                swap(other, q, "got", wc_s.at[i], wc_r.at[i], twin).wait_recv()

        each_core(go)

    def weights_sent():
        def go(which):
            swap(which, chip, "own", wz_s.at[0], wz_r.at[0], pair).wait_send()
            swap(which, chip_far, "own", wz_s.at[1], wz_r.at[1], pair).wait_send()
            swap(which, chip, "got", wf_s.at[0], wf_r.at[0], near_a).wait_send()
            swap(which, chip, "got", wf_s.at[1], wf_r.at[1], near_b).wait_send()
            for i, q in enumerate((chip, chip_a, chip_b, chip_far)):
                swap(which, q, "got", wc_s.at[i], wc_r.at[i], twin).wait_send()

        each_core(go)

    def gain_of(sub):
        return par[sub, 0:1, 0:width]

    def bias_of(sub):
        return par[sub, 1:2, 0:width]

    def mix_forward(r):
        for j in range(2 * width // 512):
            cols = pl.ds(j * 512, 512)
            sp[:, cols] = dot(hin[r], wt[:, cols]).astype(BF16)
        for t in range(chunks):
            rows = rows_of(t)
            z = (
                hin[r, rows].astype(F32)
                + dot(st[rows, 0:seq], sp[:, 0:width])
                + dot(st[rows, seq : 2 * seq], sp[:, width : 2 * width])
            )
            normed, inverse = normalize(z)
            nrm[r, rows] = normed
            inv[r, rows] = inverse
            h1[r, rows] = ((normed * gain_of(0) + bias_of(0)) * msk[r, rows]).astype(BF16)

    def inner(r, w_ref, b_row, act_ref, gp_ref, at):
        for j in range(tiles):
            cols = pl.ds(j * 512, 512)
            pre = dot(h1[r], w_ref[:, cols]) + b_row(cols)
            active, slope = gelu_pair(pre)
            act_ref[at, :, cols] = active.astype(BF16)
            gp_ref[at, :, cols] = slope.astype(BF16)

    def b_own(cols):
        return par[parity, 2:3, cols]

    def b_other(cols):
        return par[1 - parity, 2:3, cols]

    def outer_bias():
        return par[0, 3:4, 0:width] + par[1, 3:4, 0:width]

    def inner_back(r, w_ref, gp_ref, at, own):
        for j in range(tiles):
            cols = pl.ds(j * 512, 512)
            dactive = dot_cols(dzb[r], w_ref[cols, :]).astype(BF16).astype(F32)
            dpre = (dactive * gp_ref[at, :, cols].astype(F32)).astype(BF16)
            gp_ref[at, :, cols] = dpre
            if own:
                smv[2:3, cols] += jnp.sum(dpre.astype(F32), axis=0, keepdims=True)

    def ff_norm_back(r, rows, upstream, normed, inverse):
        dy = upstream.astype(F32) * msk[r, rows]
        smv[4:5, 0:width] += jnp.sum(dy * normed, axis=0, keepdims=True)
        smv[5:6, 0:width] += jnp.sum(dy, axis=0, keepdims=True)
        dz = norm_back(dy, normed, inverse, gain_of(1))
        zacc[r, rows] = dz
        rounded = dz.astype(BF16)
        dzb[r, rows] = rounded
        smv[3:4, 0:width] += jnp.sum(rounded.astype(F32), axis=0, keepdims=True)

    def mix_backward(r, upstream_ref, send):
        for t in range(chunks):
            rows = rows_of(t)
            normed = nrm[r, rows]
            dy = upstream_ref[r, rows].astype(F32) * msk[r, rows]
            smv[0:1, 0:width] += jnp.sum(dy * normed, axis=0, keepdims=True)
            smv[1:2, 0:width] += jnp.sum(dy, axis=0, keepdims=True)
            dz = norm_back(dy, normed, inv[r, rows], gain_of(0))
            zacc[r, rows] = dz
            dm[rows] = dz.astype(BF16)
        for j in range(2):
            part = dot(st[:, j * seq : (j + 1) * seq], dm[...])
            sp[:, j * width : (j + 1) * width] = part.astype(BF16)
        for t in range(chunks):
            rows = rows_of(t)
            grad = (
                zacc[r, rows]
                + dot(sp[rows, 0:width], wt[:, 0:width])
                + dot(sp[rows, width : 2 * width], wt[:, width : 2 * width])
            )
            gmix[r, rows] = grad.astype(BF16)
            if send is not None:
                send(r, t)

    def send_h(r, t, src, to):
        return remote(src.at[r, rows_of(t)], hin.at[r, rows_of(t)], h_s.at[r, t], h_r.at[r, t], to)

    def send_g(r, t, src, to):
        return remote(src.at[r, rows_of(t)], gin.at[r, rows_of(t)], g_s.at[r, t], g_r.at[r, t], to)

    def send_pa(r, t):
        return remote(hout.at[r, rows_of(t)], rxa.at[r, rows_of(t)], pa_s.at[r, t], pa_r.at[r, t], pair)

    def send_pb(r, t):
        return remote(gout.at[r, rows_of(t)], rxb.at[r, rows_of(t)], pb_s.at[r, t], pb_r.at[r, t], pair)

    def each_row(fn):
        def step(r, carry):
            fn(r)
            return carry

        lax.fori_loop(0, n_rows, step, 0)

    @pl.when(section < 2)
    def _():
        load_x.wait()
        load_wt.wait()
        load_st.wait()
        swap_par.wait()
        load_w1.wait()
        load_w2.wait()

        def row(r):
            hin[r] = (hin[r].astype(F32) * msk[r]).astype(BF16)
            mix_forward(r)
            inner(r, w1, b_own, act, gp, r)

            @pl.when(section == 0)
            def _():
                for t in range(chunks):
                    rows = rows_of(t)
                    hout[r, rows] = dot(act[r, rows], w2[...]).astype(BF16)
                    send_pa(r, t).start()

            @pl.when(section == 1)
            def _():
                for t in range(chunks):
                    rows = rows_of(t)
                    zacc[r, rows] = h1[r, rows].astype(F32) + dot(act[r, rows], w2[...]) + outer_bias()
                for t in range(chunks):
                    rows = rows_of(t)
                    send_pa(r, t).wait_recv()
                    normed, inverse = normalize(zacc[r, rows] + rxa[r, rows].astype(F32))
                    nrm[r, rows] = normed
                    inv[r, rows] = inverse
                    hout[r, rows] = ((normed * gain_of(1) + bias_of(1)) * msk[r, rows]).astype(BF16)
                    send_h(r, t, hout, up).start()

        each_row(row)

    @pl.when(section >= 2)
    def _():
        weights_begin()
        load_wt.wait()
        load_st.wait()
        load_cot.wait()
        swap_par.wait()
        weights_spread()

        def row(r):
            for t in range(chunks):
                send_h(r, t, hin, up).wait_recv()

                @pl.when(section == 2)
                def _():
                    send_h(r, t, hin, up).start()

            mix_forward(r)
            inner(r, w1, b_own, act, gp, r)
            pl.when(r == 0)(weights_end)
            inner(r, w1x, b_other, actx, gpx, 0)
            for t in range(chunks):
                rows = rows_of(t)
                z = (
                    h1[r, rows].astype(F32)
                    + dot(act[r, rows], w2[...])
                    + dot(actx[0, rows], w2x[...])
                    + outer_bias()
                )
                normed, inverse = normalize(z)
                hout[r, rows] = ((normed * gain_of(1) + bias_of(1)) * msk[r, rows]).astype(BF16)
                ff_norm_back(r, rows, gin[r, rows], normed, inverse)
            inner_back(r, w2, gp, r, True)
            inner_back(r, w2x, gpx, 0, False)
            for t in range(chunks):
                rows = rows_of(t)
                grad = zacc[r, rows] + dot_cols(gp[r, rows], w1[...]) + dot_cols(gpx[0, rows], w1x[...])
                gout[r, rows] = grad.astype(BF16)

            @pl.when(section == 2)
            def _():
                mix_backward(r, gout, lambda r, t: send_g(r, t, gmix, down).start())

        each_row(row)

    def take_pb(r):
        for t in range(chunks):
            rows = rows_of(t)
            send_pb(r, t).wait_recv()
            gout[r, rows] = (zacc[r, rows] + rxb[r, rows].astype(F32)).astype(BF16)
            send_pb(r, t).start()

    @pl.when(section == 1)
    def _():
        def row(r):
            pl.when(r > 0)(lambda: take_pb(r - 1))
            for t in range(chunks):
                rows = rows_of(t)
                send_g(r, t, dzb, down).wait_recv()
                ff_norm_back(r, rows, gin[r, rows], nrm[r, rows], inv[r, rows])
                send_g(r, t, dzb, down).start()
            inner_back(r, w2, gp, r, True)
            for t in range(chunks):
                rows = rows_of(t)
                zacc[r, rows] += dot_cols(gp[r, rows], w1[...])

        each_row(row)

    @pl.when(section == 0)
    def _():
        def row(r):
            for t in range(chunks):
                rows = rows_of(t)
                send_g(r, t, dzb, up).wait_recv()
                dzb[r, rows] = gin[r, rows]
                smv[3:4, 0:width] += jnp.sum(gin[r, rows].astype(F32), axis=0, keepdims=True)
            inner_back(r, w2, gp, r, True)
            for t in range(chunks):
                rows = rows_of(t)
                gout[r, rows] = dot_cols(gp[r, rows], w1[...]).astype(BF16)
                send_pb(r, t).start()

        each_row(row)

    def store_so(src):
        return pltpu.make_async_copy(src, so_hbm, s_out.at[0])

    def store_ig(src):
        return pltpu.make_async_copy(src, ig_hbm, s_out.at[1])

    pl.when(parity == 0)(lambda: store_so(h1).start())
    pl.when(parity == 1)(lambda: store_so(hout).start())
    pl.when(section == 2)(lambda: store_ig(gmix).start())
    pl.when(section == 3)(lambda: store_ig(gout).start())

    def quarters(a, b):
        return [
            ((1 - a) * 2 + (1 - b)) * quarter,
            ((1 - a) * 2 + b) * quarter,
            (a * 2 + (1 - b)) * quarter,
            (a * 2 + b) * quarter,
        ]

    offs_1 = quarters(bit_value[0], bit_value[1])
    offs_2 = quarters(bit_value[levels - 1], bit_value[levels - 2])
    offs = [by_core(a, b) for a, b in zip(offs_1, offs_2)]
    offs_x = [by_core(b, a) for a, b in zip(offs_1, offs_2)]

    def piece(offset, count):
        return pl.ds(pl.multiple_of(offset, 16), count)

    def lanes(offset):
        return pl.ds(pl.multiple_of(offset, 128), quarter)

    def to_twin(i, offset):
        return remote(G.at[1, piece(offset, quarter)], RC.at[piece(offset, quarter)], rc_s.at[i], rc_r.at[i], twin)

    def first_hop(i):
        return remote(G.at[0, piece(offs[i], quarter)], R1.at[i], r1_s.at[i], r1_r.at[i], peer[0])

    def fold_twin(i):
        to_twin(i, offs[i]).wait_recv()
        rows = piece(offs[i], quarter)
        G[0, rows] = (G[0, rows].astype(F32) + RC[rows].astype(F32)).astype(BF16)
        if i < 2:
            first_hop(i).start()

    for i in range(4):
        grad_1 = dot_rows(gp[0, :, lanes(offs_1[i])], h1[0])
        grad_2 = dot_rows(act[0, :, lanes(offs_2[i])], dzb[0])
        for r in range(1, n_rows):
            grad_1 += dot_rows(gp[r, :, lanes(offs_1[i])], h1[r])
            grad_2 += dot_rows(act[r, :, lanes(offs_2[i])], dzb[r])
        G[core, piece(offs_1[i], quarter)] = grad_1.astype(BF16)
        G[1 - core, piece(offs_2[i], quarter)] = grad_2.astype(BF16)
        to_twin(i, offs_x[i]).start()
        if i > 0:
            fold_twin(i - 1)
    fold_twin(3)

    @pl.when(section == 1)
    def _():
        take_pb(n_rows - 1)
        store_ig(gout).start()

    def fold_first(i):
        first_hop(i).wait_recv()
        rows = piece(offs[2 + i], quarter)
        G[0, rows] = (G[0, rows].astype(F32) + R1[i].astype(F32)).astype(BF16)

    def later_hop(k, src_offset, count):
        return remote(
            G.at[0, piece(src_offset, count)], R2.at[k - 1, pl.ds(0, count)], r2_s.at[k - 1], r2_r.at[k - 1], peer[k]
        )

    fold_first(0)
    later_hop(1, offs[2], quarter).start()
    fold_first(1)
    later_hop(1, offs[2], quarter).wait_recv()
    rows = piece(offs[3], quarter)
    G[0, rows] = (G[0, rows].astype(F32) + R2[0].astype(F32)).astype(BF16)
    keep = [offs[3]]
    sent_later = [later_hop(1, offs[2], quarter)]
    count = quarter
    for k in range(2, levels):
        count //= 2
        away = keep[-1] + (1 - value[k]) * count
        keep.append(keep[-1] + value[k] * count)
        hop = later_hop(k, away, count)
        hop.start()
        hop.wait_recv()
        rows = piece(keep[-1], count)
        G[0, rows] = (G[0, rows].astype(F32) + R2[k - 1, pl.ds(0, count)].astype(F32)).astype(BF16)
        sent_later.append(hop)

    def spread(src, offset, count, i, device):
        return remote(src, gw_hbm.at[core, piece(offset, count)], ag_s.at[i], ag_r.at[i], device)

    def final_at(offset, count):
        return gw_hbm.at[core, piece(offset, count)]

    own_out = pltpu.make_async_copy(G.at[0, piece(keep[-1], count)], final_at(keep[-1], count), s_out.at[2])
    own_out.start()
    spare = []
    if levels > 2:
        own_out.wait()
        for k in range(levels - 1, 1, -1):
            mine = keep[k - 1]
            copy = spread(final_at(mine, count), mine, count, 2 + k, peer[k])
            copy.start()
            copy.wait_recv()
            spare.append(copy)
            count *= 2
        source = final_at(offs[3], quarter)
    else:
        source = G.at[0, piece(offs[3], quarter)]

    def chip_copy(i, src, offset):
        return remote(src, gw_hbm.at[core, piece(offset, quarter)], oc_s.at[i], oc_r.at[i], twin)

    own_1 = spread(source, offs[3], quarter, 0, peer[1])
    own_0 = spread(source, offs[3], quarter, 1, peer[0])
    own_1.start()
    own_0.start()
    out_3 = chip_copy(3, source, offs[3])
    out_3.start()

    @pl.when(section == 0)
    def _():
        for t in range(chunks):
            send_pb(0, t).wait_recv()
        mix_backward(0, rxb, None)

    own_1.wait_recv()
    pass_0 = spread(final_at(offs[2], quarter), offs[2], quarter, 2, peer[0])
    pass_0.start()
    out_2 = chip_copy(2, final_at(offs[2], quarter), offs[2])
    out_2.start()

    @pl.when(section == 0)
    def _():
        for r in range(1, n_rows):
            for t in range(chunks):
                send_pb(r, t).wait_recv()
            mix_backward(r, rxb, None)
        store_ig(gmix).start()

    @pl.when(parity == 1)
    def _():
        smv[0:2] = smv[4:6]

    small_hops = []
    for k in range(levels + 1):
        to = twin if k == 0 else peer[k - 1]
        sms[k] = smv[...]
        hop = remote(sms.at[k], smr.at[k], sm_s.at[k], sm_r.at[k], to)
        hop.start()
        hop.wait_recv()
        smv[...] += smr[k]
        small_hops.append(hop)
    small_ref[...] = smv[...]

    own_0.wait_recv()
    out_1 = chip_copy(1, final_at(offs[1], quarter), offs[1])
    out_1.start()
    pass_0.wait_recv()
    out_0 = chip_copy(0, final_at(offs[0], quarter), offs[0])
    out_0.start()
    for copy in (out_3, out_2, out_1, out_0):
        copy.wait_recv()

    for copy in [own_1, own_0, pass_0, out_3, out_2, out_1, out_0, first_hop(0), first_hop(1)]:
        copy.wait_send()
    for copy in sent_later + small_hops + spare:
        copy.wait_send()
    for i in range(4):
        to_twin(i, offs_x[i]).wait_send()
    if levels == 2:
        own_out.wait()
    store_so(h1).wait()
    store_ig(gout).wait()

    def sent(*makers):
        for r in range(n_rows):
            for t in range(chunks):
                for make in makers:
                    make(r, t).wait_send()

    pl.when(section == 0)(lambda: sent(send_pa, send_pb))
    pl.when(section == 1)(lambda: sent(lambda r, t: send_h(r, t, hout, up), lambda r, t: send_g(r, t, dzb, down), send_pb))

    @pl.when(section == 2)
    def _():
        sent(lambda r, t: send_h(r, t, hin, up), lambda r, t: send_g(r, t, gmix, down))

    pl.when(section >= 2)(weights_sent)


def per_device(block_input, out_cotangent, lengths, ln_gain, ln_bias, w_in, b_in, w_out, b_out):
    n_rows, seq, width = block_input.shape
    half = w_in.shape[2]
    dp_count = lax.axis_size("dp")
    levels = int(math.log2(dp_count)) - 1
    chunks = seq // CHUNK
    quarter = half // 4
    cos_w, sin_w = dft_pair(width)
    cos_s, sin_s = dft_pair(seq)
    wt = jnp.asarray(np.concatenate([cos_w, sin_w], axis=1).astype(ml_dtypes.bfloat16))
    st = jnp.asarray(np.concatenate([cos_s, -sin_s], axis=1).astype(ml_dtypes.bfloat16))
    row_block = (n_rows, seq, width)
    dma = pltpu.SemaphoreType.DMA
    vmem = pl.BlockSpec(memory_space=pltpu.VMEM)
    anywhere = pl.BlockSpec(memory_space=pl.ANY)
    by_chunk = [dma((n_rows, chunks))] * 8
    scratch = [
        pltpu.VMEM((width, half), BF16),
        pltpu.VMEM((half, width), BF16),
        pltpu.VMEM((width, half), BF16),
        pltpu.VMEM((half, width), BF16),
        pltpu.VMEM((width, 2 * width), BF16),
        pltpu.VMEM((seq, 2 * seq), BF16),
        *[pltpu.VMEM(row_block, BF16) for _ in range(9)],
        pltpu.VMEM((n_rows, seq, half), BF16),
        pltpu.VMEM((n_rows, seq, half), BF16),
        pltpu.VMEM((1, seq, half), BF16),
        pltpu.VMEM((1, seq, half), BF16),
        pltpu.VMEM((seq, 2 * width), BF16),
        pltpu.VMEM((seq, width), BF16),
        pltpu.VMEM(row_block, F32),
        pltpu.VMEM(row_block, F32),
        pltpu.VMEM((n_rows, seq, 1), F32),
        pltpu.VMEM((n_rows, seq, 1), F32),
        pltpu.VMEM((2, 8, half), F32),
        pltpu.VMEM((2, half, width), BF16),
        pltpu.VMEM((half, width), BF16),
        pltpu.VMEM((2, quarter, width), BF16),
        pltpu.VMEM((levels - 1, quarter, width), BF16),
        pltpu.VMEM((levels + 1, 8, half), F32),
        pltpu.VMEM((levels + 1, 8, half), F32),
        pltpu.VMEM((8, half), F32),
        dma((6,)),
        dma((3,)),
        dma,
        dma,
        *by_chunk,
        dma((2,)),
        dma((2,)),
        dma((2,)),
        dma((2,)),
        dma((4,)),
        dma((4,)),
        dma((4,)),
        dma((4,)),
        dma((2,)),
        dma((2,)),
        dma((levels - 1,)),
        dma((levels - 1,)),
        dma((levels + 2,)),
        dma((levels + 2,)),
        dma((4,)),
        dma((4,)),
        dma((levels + 1,)),
        dma((levels + 1,)),
    ]
    section_out, input_grad, weight_grad, small = pl.pallas_call(
        functools.partial(relay, dp_count),
        out_shape=(
            jax.ShapeDtypeStruct(row_block, BF16),
            jax.ShapeDtypeStruct(row_block, BF16),
            jax.ShapeDtypeStruct((2, half, width), BF16),
            jax.ShapeDtypeStruct((8, half), F32),
        ),
        in_specs=[
            pl.BlockSpec(memory_space=pltpu.SMEM),
            anywhere,
            anywhere,
            vmem,
            vmem,
            vmem,
            vmem,
            anywhere,
            anywhere,
            anywhere,
            anywhere,
        ],
        out_specs=(anywhere, anywhere, anywhere, vmem),
        scratch_shapes=scratch,
        compiler_params=pltpu.CompilerParams(
            collective_id=0, has_side_effects=True, vmem_limit_bytes=62 * 2**20
        ),
        name="fnet_relay",
    )(lengths, block_input, out_cotangent, ln_gain, ln_bias, b_in, b_out, w_in[0], w_out[0], wt, st)
    odd = lax.axis_index("section") % 2
    b_out_grad = lax.dynamic_slice(small, (3, odd * (width // 2)), (1, width // 2))
    return (
        section_out[None],
        input_grad.astype(F32)[None],
        small[0:1, 0:width],
        small[1:2, 0:width],
        weight_grad[0].T.astype(F32)[None],
        small[2:3, :],
        weight_grad[1].astype(F32)[None],
        b_out_grad,
    )


def solution(mesh):
    in_specs = (
        P("dp", None, None),
        P("dp", None, None),
        P("dp"),
        P("section", None),
        P("section", None),
        P("section", None, None),
        P("section", None),
        P("section", None, None),
        P("section", None),
    )
    out_specs = (
        P("section", "dp", None, None),
        P("section", "dp", None, None),
        P("section", None),
        P("section", None),
        P("section", None, None),
        P("section", None),
        P("section", None, None),
        P("section", None),
    )
    return jax.shard_map(
        per_device, mesh=mesh, in_specs=in_specs, out_specs=out_specs, check_vma=False
    )
```

```python
import functools
import math

import jax
import jax.numpy as jnp
import ml_dtypes
import numpy as np
from jax import lax
from jax.experimental import pallas as pl
from jax.experimental.pallas import tpu as pltpu
from jax.sharding import PartitionSpec as P

MESH = pl.DeviceIdType.MESH
F32, BF16 = jnp.float32, jnp.bfloat16
EPS = 1e-05
CHUNK = 128
WIDE = 2
ROOT_HALF = 1.0 / math.sqrt(2.0)
PDF_SCALE = 1.0 / math.sqrt(2.0 * math.pi)


def dft_pair(length):
    positions = np.arange(length, dtype=np.int64)
    angle = (positions[:, None] * positions[None, :] % length) * (2.0 * math.pi / length)
    scale = 1.0 / math.sqrt(length)
    return np.cos(angle) * scale, np.sin(angle) * scale


def dot(a, b):
    return jnp.dot(a, b, preferred_element_type=F32)


def dot_cols(a, b):
    return lax.dot_general(a, b, (((1,), (1,)), ((), ())), preferred_element_type=F32)


def dot_rows(a, b):
    return lax.dot_general(a, b, (((0,), (0,)), ((), ())), preferred_element_type=F32)


def gelu_pair(v):
    cdf = 0.5 * (1.0 + lax.erf(v * ROOT_HALF))
    return v * cdf, cdf + v * (jnp.exp(-0.5 * v * v) * PDF_SCALE)


def normalize(z):
    centre = z - jnp.mean(z, axis=-1, keepdims=True)
    spread = jnp.mean(centre * centre, axis=-1, keepdims=True)
    inverse = lax.rsqrt(spread + EPS)
    return centre * inverse, inverse


def norm_back(dy, normed, inverse, gain):
    e = dy * gain
    return inverse * (
        e - jnp.mean(e, axis=-1, keepdims=True) - normed * jnp.mean(e * normed, axis=-1, keepdims=True)
    )


def remote(src, dst, send, recv, device):
    return pltpu.make_async_remote_copy(
        src_ref=src, dst_ref=dst, send_sem=send, recv_sem=recv, device_id=device, device_id_type=MESH
    )


def relay(
    dp_count,
    lengths, x_hbm, cot_hbm, gain_ref, bias_ref, b_in_ref, b_out_ref, w1_hbm, w2_hbm, wt_hbm, st_hbm,
    so_hbm, ig_hbm, gw_hbm, small_ref,
    w1, w2, w1x, w2x, wt, st, hin, gin, rxa, rxb, h1, hout, dzb, gout, gmix, act, gp, actx, gpx, sp, dm,
    zacc, nrm, inv, msk, par, G, RC, R1, R2, sms, smr, smv,
    turn, s_load, s_out, par_s, par_r, h_s, h_r, g_s, g_r, pa_s, pa_r, pb_s, pb_r,
    wz_s, wz_r, wa_s, wa_r, wb_s, wb_r, wc_s, wc_r, rc_s, rc_r, r1_s, r1_r, r2_s, r2_r, ag_s, ag_r, oc_s, oc_r, lo_s, lo_r, sm_s, sm_r,
):
    section = lax.axis_index("section")
    d = lax.axis_index("dp")
    core = lax.rem(d, 2)
    parity = lax.rem(section, 2)
    n_rows, seq, width = hin.shape
    half = w1.shape[1]
    chunks = seq // CHUNK
    tiles = half // 512
    levels = int(math.log2(dp_count)) - 1
    bits = [2 << k for k in range(levels)]

    def flipped(bit):
        return d + bit - 2 * bit * lax.rem(d // bit, 2)

    def by_core(first, second):
        return first + core * (second - first)

    bit_value = [lax.rem(d // b, 2) for b in bits]
    value = [by_core(bit_value[k], bit_value[levels - 1 - k]) for k in range(levels)]
    peer = [(section, by_core(flipped(bits[k]), flipped(bits[levels - 1 - k]))) for k in range(levels)]
    twin = (section, d + 1 - 2 * core)
    pair = (section + 1 - 2 * parity, d)
    up = (section + 1, d)
    down = (section - 1, d)

    def rows_of(t):
        return pl.ds(t * CHUNK, CHUNK)

    wide_rows = [pl.ds(i * WIDE * CHUNK, WIDE * CHUNK) for i in range(chunks // WIDE)]

    barrier = pltpu.get_barrier_semaphore()

    def greet(device):
        pl.semaphore_signal(barrier, inc=1, device_id=device, device_id_type=MESH)

    greet(twin)
    for k in range(levels):
        greet(peer[k])
    pl.when(section > 0)(lambda: greet(down))
    pl.when(section < 3)(lambda: greet(up))

    load_x = pltpu.make_async_copy(x_hbm, hin, s_load.at[0])
    load_cot = pltpu.make_async_copy(cot_hbm, gin, s_load.at[1])
    load_wt = pltpu.make_async_copy(wt_hbm, wt, s_load.at[2])
    load_st = pltpu.make_async_copy(st_hbm, st, s_load.at[3])
    load_w1 = pltpu.make_async_copy(w1_hbm, w1, s_load.at[4])
    load_w2 = pltpu.make_async_copy(w2_hbm, w2, s_load.at[5])

    @pl.when(section < 2)
    def _():
        load_x.start()
        load_wt.start()
        load_st.start()
        load_w1.start()
        load_w2.start()

    @pl.when(section >= 2)
    def _():
        load_w1.start()
        load_w2.start()
        load_wt.start()
        load_st.start()
        load_cot.start()

    par[parity] = jnp.zeros(par.shape[1:], F32)
    par[parity, 0:1, 0:width] = gain_ref[...]
    par[parity, 1:2, 0:width] = bias_ref[...]
    par[parity, 2:3, :] = b_in_ref[...].astype(F32)
    par[parity, 3:4, pl.ds(pl.multiple_of(parity * (width // 2), 128), width // 2)] = b_out_ref[...].astype(F32)
    smv[...] = jnp.zeros(smv.shape, F32)
    for r in range(n_rows):
        position = lax.broadcasted_iota(jnp.int32, (seq, 1), 0)
        msk[r] = jnp.where(position < lengths[r], 1.0, 0.0).astype(F32)

    pl.semaphore_wait(barrier, 1 + levels + jnp.where((section == 0) | (section == 3), 1, 2))

    swap_par = remote(par.at[parity], par.at[parity], par_s, par_r, pair)
    swap_par.start()

    quarter = half // 4
    chip = lax.rem(d // 2, 4)
    chip_far = 3 - chip
    chip_a = chip + 1 - 2 * lax.rem(chip, 2)
    chip_b = 3 - chip_a
    near_a = (section, flipped(2))
    near_b = (section, flipped(4))

    def swap(which, q, i, n, own, send, recv, device):
        if which == 0:
            from_ref, to_ref = (w1_hbm if own else w1x), w1x
        else:
            from_ref, to_ref = (w2_hbm if own else w2x), w2x
        third = to_ref.shape[0] // 12
        part = pl.ds(pl.multiple_of((3 * q + i) * third, 16), n * third)
        return remote(from_ref.at[part], to_ref.at[part], send, recv, device)

    def each_core(fn):
        for which in range(2):
            pl.when(core == which)(functools.partial(fn, which))

    def z_hop(which, i):
        if i < 3:
            return swap(which, chip, i, 1, True, wz_s.at[i], wz_r.at[i], pair)
        return swap(which, chip_far, 0, 1, True, wz_s.at[3], wz_r.at[3], pair)

    def a_hop(which, i):
        if i < 3:
            return swap(which, chip, i, 1, False, wa_s.at[i], wa_r.at[i], near_a)
        return swap(which, chip_b, 1, 1, False, wa_s.at[3], wa_r.at[3], near_a)

    def b_hop(which, i):
        if i < 3:
            return swap(which, chip, i, 1, False, wb_s.at[i], wb_r.at[i], near_b)
        return swap(which, chip_a, 2, 1, False, wb_s.at[3], wb_r.at[3], near_b)

    def a_got(which, i):
        if i < 3:
            return swap(which, chip_a, i, 1, False, wa_s.at[i], wa_r.at[i], near_a)
        return swap(which, chip_far, 1, 1, False, wa_s.at[3], wa_r.at[3], near_a)

    def b_got(which, i):
        if i < 3:
            return swap(which, chip_b, i, 1, False, wb_s.at[i], wb_r.at[i], near_b)
        return swap(which, chip_far, 2, 1, False, wb_s.at[3], wb_r.at[3], near_b)

    def twin_hop(which, i):
        q = (chip, chip_a, chip_b, chip_far)[i]
        return swap(which, q, 0, 3, False, wc_s.at[i], wc_r.at[i], twin)

    def weights_begin():
        def go(which):
            for i in range(4):
                z_hop(which, i).start()

        each_core(go)

    def weights_spread():
        def go(which):
            for i in range(3):
                z_hop(which, i).wait_recv()
                a_hop(which, i).start()
                b_hop(which, i).start()
            twin_hop(which, 0).start()
            b_got(which, 0).wait_recv()
            b_got(which, 1).wait_recv()
            a_hop(which, 3).start()
            for i in range(3):
                a_got(which, i).wait_recv()
            b_hop(which, 3).start()
            twin_hop(which, 1).start()

        each_core(go)

    def weights_end():
        def go(which):
            b_got(which, 2).wait_recv()
            twin_hop(which, 2).start()
            z_hop(which, 3).wait_recv()
            a_got(which, 3).wait_recv()
            b_got(which, 3).wait_recv()
            twin_hop(which, 3).start()

        each_core(go)

    def weights_ready():
        def go(which):
            for i in range(4):
                twin_hop(1 - which, i).wait_recv()

        each_core(go)

    def weights_sent():
        def go(which):
            for i in range(4):
                pl.when(section > 0)(z_hop(which, i).wait_send)

                @pl.when(section != 1)
                def _():
                    a_hop(which, i).wait_send()
                    b_hop(which, i).wait_send()
                    twin_hop(which, i).wait_send()

        each_core(go)

    def gain_of(sub):
        return par[sub, 0:1, 0:width]

    def bias_of(sub):
        return par[sub, 1:2, 0:width]

    def mix_forward(r):
        for j in range(2 * width // 512):
            cols = pl.ds(j * 512, 512)
            sp[:, cols] = dot(hin[r], wt[:, cols]).astype(BF16)
        for t in range(chunks):
            rows = rows_of(t)
            z = (
                hin[r, rows].astype(F32)
                + dot(st[rows, 0:seq], sp[:, 0:width])
                + dot(st[rows, seq : 2 * seq], sp[:, width : 2 * width])
            )
            normed, inverse = normalize(z)
            nrm[r, rows] = normed
            inv[r, rows] = inverse
            h1[r, rows] = ((normed * gain_of(0) + bias_of(0)) * msk[r, rows]).astype(BF16)

    def inner(r, w_ref, b_row, act_ref, act_at, gp_ref):
        for j in range(tiles):
            cols = pl.ds(j * 512, 512)
            for t in range(chunks):
                rows = rows_of(t)
                pre = dot(h1[r, rows], w_ref[:, cols]) + b_row(cols)
                active, slope = gelu_pair(pre)
                act_ref[act_at, rows, cols] = active.astype(BF16)
                gp_ref[r, rows, cols] = slope.astype(BF16)

    def b_own(cols):
        return par[parity, 2:3, cols]

    def b_other(cols):
        return par[1 - parity, 2:3, cols]

    def outer_bias():
        return par[0, 3:4, 0:width] + par[1, 3:4, 0:width]

    def inner_back(r, w_ref, gp_ref, own):
        for j in range(tiles):
            cols = pl.ds(j * 512, 512)
            dactive = dot_cols(dzb[r], w_ref[cols, :]).astype(BF16).astype(F32)
            dpre = (dactive * gp_ref[r, :, cols].astype(F32)).astype(BF16)
            gp_ref[r, :, cols] = dpre
            if own:
                smv[2:3, cols] += jnp.sum(dpre.astype(F32), axis=0, keepdims=True)

    def ff_norm_back(r, rows, upstream, normed, inverse):
        dy = upstream.astype(F32) * msk[r, rows]
        smv[4:5, 0:width] += jnp.sum(dy * normed, axis=0, keepdims=True)
        smv[5:6, 0:width] += jnp.sum(dy, axis=0, keepdims=True)
        dz = norm_back(dy, normed, inverse, gain_of(1))
        zacc[r, rows] = dz
        rounded = dz.astype(BF16)
        dzb[r, rows] = rounded
        smv[3:4, 0:width] += jnp.sum(rounded.astype(F32), axis=0, keepdims=True)

    def mix_backward(r, upstream_ref):
        for t in range(chunks):
            rows = rows_of(t)
            normed = nrm[r, rows]
            dy = upstream_ref[r, rows].astype(F32) * msk[r, rows]
            smv[0:1, 0:width] += jnp.sum(dy * normed, axis=0, keepdims=True)
            smv[1:2, 0:width] += jnp.sum(dy, axis=0, keepdims=True)
            dz = norm_back(dy, normed, inv[r, rows], gain_of(0))
            zacc[r, rows] = dz
            dm[rows] = dz.astype(BF16)
        for j in range(2):
            part = dot(st[:, j * seq : (j + 1) * seq], dm[...])
            sp[:, j * width : (j + 1) * width] = part.astype(BF16)
        for t in range(chunks):
            rows = rows_of(t)
            grad = (
                zacc[r, rows]
                + dot(sp[rows, 0:width], wt[:, 0:width])
                + dot(sp[rows, width : 2 * width], wt[:, width : 2 * width])
            )
            gmix[r, rows] = grad.astype(BF16)
            pl.when(section == 2)(send_g(r, t, gmix, down).start)

    def send_h(r, t, src, to):
        return remote(src.at[r, rows_of(t)], hin.at[r, rows_of(t)], h_s.at[r, t], h_r.at[r, t], to)

    def send_g(r, t, src, to):
        return remote(src.at[r, rows_of(t)], gin.at[r, rows_of(t)], g_s.at[r, t], g_r.at[r, t], to)

    def send_pa(r, t):
        return remote(hout.at[r, rows_of(t)], rxa.at[r, rows_of(t)], pa_s.at[r, t], pa_r.at[r, t], pair)

    def send_pb(r, t, src):
        return remote(src.at[r, rows_of(t)], rxb.at[r, rows_of(t)], pb_s.at[r, t], pb_r.at[r, t], pair)

    first_layer = section < 2
    whole = section != 1

    def finish_with_pair(r):
        for t in range(chunks):
            rows = rows_of(t)
            send_pa(r, t).wait_recv()
            normed, inverse = normalize(zacc[r, rows] + rxa[r, rows].astype(F32))
            nrm[r, rows] = normed
            inv[r, rows] = inverse
            hout[r, rows] = ((normed * gain_of(1) + bias_of(1)) * msk[r, rows]).astype(BF16)
            send_h(r, t, hout, up).start()

    def row_forward(r):
        @pl.when(first_layer)
        def _():
            hin[r] = (hin[r].astype(F32) * msk[r]).astype(BF16)

        @pl.when(jnp.logical_not(first_layer))
        def _():
            for t in range(chunks):
                send_h(r, t, hin, up).wait_recv()
                pl.when(section == 2)(send_h(r, t, hin, up).start)

        mix_forward(r)
        inner(r, w1, b_own, act, r, gp)

        @pl.when(first_layer)
        def _():
            for t in range(chunks):
                rows = rows_of(t)
                part = dot(act[r, rows], w2[...])

                @pl.when(section == 0)
                def _():
                    hout[r, rows] = part.astype(BF16)
                    pl.when((core == 0) & (r == 0))(send_pa(r, t).start)

                @pl.when(section == 1)
                def _():
                    zacc[r, rows] = h1[r, rows].astype(F32) + part + outer_bias()

        pl.when(section == 1)(lambda: finish_with_pair(r))

    def send_row(r):
        for t in range(chunks):
            send_pa(r, t).start()

    def half_sent(r):
        for t in range(chunks // 2):
            send_pa(r, t).wait_send()

    def hand_over(r):
        half_sent(r)
        pl.semaphore_signal(turn, inc=1, device_id=twin, device_id_type=MESH)

    def take_turns():
        @pl.when(core == 0)
        def _():
            hand_over(0)
            for r in range(1, n_rows):
                pl.semaphore_wait(turn, 1)
                send_row(r)
                hand_over(r)

        @pl.when(core == 1)
        def _():
            for r in range(n_rows):
                pl.semaphore_wait(turn, 1)
                send_row(r)
                (hand_over if r < n_rows - 1 else half_sent)(r)

    def part_back(r):
        for i, rows in enumerate(wide_rows):
            part = dot_cols(gp[r, rows], w1[...])

            @pl.when(section == 0)
            def _():
                zacc[r, rows] = dzb[r, rows].astype(F32)
                rxa[r, rows] = part.astype(BF16)
                for t in range(i * WIDE, (i + 1) * WIDE):
                    send_pb(r, t, rxa).start()

            zacc[r, rows] += part

            @pl.when(whole)
            def _():
                gout[r, rows] = (zacc[r, rows] + dot_cols(gpx[r, rows], w1x[...])).astype(BF16)

    def row_backward(r):
        pl.when((section == 0) & (r == 0))(weights_spread)
        pl.when(((section == 0) | ((section > 1) & (core == 0))) & (r == 0))(weights_end)
        pl.when(whole & (r == 0))(weights_ready)
        pl.when(whole)(lambda: inner(r, w1x, b_other, actx, 0, gpx))

        @pl.when(section == 0)
        def _():
            for t in range(chunks):
                rows = rows_of(t)
                send_g(r, t, dzb, up).wait_recv()
                dzb[r, rows] = gin[r, rows]
                smv[3:4, 0:width] += jnp.sum(gin[r, rows].astype(F32), axis=0, keepdims=True)

        @pl.when(section == 1)
        def _():
            for t in range(chunks):
                rows = rows_of(t)
                send_g(r, t, dzb, down).wait_recv()
                ff_norm_back(r, rows, gin[r, rows], nrm[r, rows], inv[r, rows])
                send_g(r, t, dzb, down).start()

        @pl.when(jnp.logical_not(first_layer))
        def _():
            for t in range(chunks):
                rows = rows_of(t)
                z = (
                    h1[r, rows].astype(F32)
                    + dot(act[r, rows], w2[...])
                    + dot(actx[0, rows], w2x[...])
                    + outer_bias()
                )
                normed, inverse = normalize(z)
                hout[r, rows] = ((normed * gain_of(1) + bias_of(1)) * msk[r, rows]).astype(BF16)
                ff_norm_back(r, rows, gin[r, rows], normed, inverse)

        inner_back(r, w2, gp, True)

        pl.when(whole)(lambda: inner_back(r, w2x, gpx, False))

    def join_parts(r, to):
        for t in range(chunks):
            rows = rows_of(t)
            send_pb(r, t, rxa).wait_recv()
            to[r, rows] = (zacc[r, rows] + rxb[r, rows].astype(F32)).astype(BF16)

    pl.when(section > 0)(weights_begin)
    load_wt.wait()
    load_st.wait()
    load_w1.wait()
    load_w2.wait()
    swap_par.wait()

    @pl.when(first_layer)
    def _():
        load_x.wait()

    @pl.when(jnp.logical_not(first_layer))
    def _():
        load_cot.wait()
        weights_spread()
        pl.when(core == 1)(weights_end)

    def store_so(src):
        return pltpu.make_async_copy(src, so_hbm, s_out.at[0])

    def store_ig(src):
        return pltpu.make_async_copy(src, ig_hbm, s_out.at[1])

    def store_ready():
        pl.when(parity == 0)(lambda: store_so(h1).start())
        pl.when(parity == 1)(lambda: store_so(hout).start())
        pl.when(section == 2)(lambda: store_ig(gmix).start())
        pl.when(section == 3)(lambda: store_ig(gout).start())

    def place(a, b, i):
        first, second = i // 2, lax.rem(i, 2)
        return ((1 - a + first * (2 * a - 1)) * 2 + 1 - b + second * (2 * b - 1)) * quarter

    def place_1(i):
        return place(bit_value[0], bit_value[1], i)

    def place_2(i):
        return place(bit_value[levels - 1], bit_value[levels - 2], i)

    def place_own(i):
        return by_core(place_1(i), place_2(i))

    def place_twin(i):
        return by_core(place_2(i), place_1(i))

    offs = [place_own(i) for i in range(4)]

    def piece(offset, count):
        return pl.ds(pl.multiple_of(offset, 16), count)

    def lanes(offset):
        return pl.ds(pl.multiple_of(offset, 128), quarter)

    def to_twin(i, offset):
        return remote(G.at[1, piece(offset, quarter)], RC.at[piece(offset, quarter)], rc_s.at[i], rc_r.at[i], twin)

    def first_hop(i):
        return remote(G.at[0, piece(place_own(i), quarter)], R1.at[i], r1_s.at[i], r1_r.at[i], peer[0])

    def fold_twin(i):
        to_twin(i, place_own(i)).wait_recv()
        rows = piece(place_own(i), quarter)
        G[0, rows] = (G[0, rows].astype(F32) + RC[rows].astype(F32)).astype(BF16)

    def grads_quarter(i):
        at_1, at_2 = place_1(i), place_2(i)
        grad_1 = dot_rows(gp[0, :, lanes(at_1)], h1[0])
        grad_2 = dot_rows(act[0, :, lanes(at_2)], dzb[0])
        for r in range(1, n_rows):
            grad_1 += dot_rows(gp[r, :, lanes(at_1)], h1[r])
            grad_2 += dot_rows(act[r, :, lanes(at_2)], dzb[r])
        G[core, piece(at_1, quarter)] = grad_1.astype(BF16)
        G[1 - core, piece(at_2, quarter)] = grad_2.astype(BF16)
        to_twin(i, place_twin(i)).start()

    def grads():
        for i in range(4):
            pl.when(section > 0)(lambda: small_begin(i) if i <= levels else None)
            grads_quarter(i)
            if i > 0:
                fold_twin(i - 1)
            if 1 <= i < 3:
                first_hop(i - 1).start()
            pl.when(section > 0)(lambda: small_end(i) if i <= levels else None)
        fold_twin(3)

    def fold_first(i):
        first_hop(i).wait_recv()
        rows = piece(offs[2 + i], quarter)
        G[0, rows] = (G[0, rows].astype(F32) + R1[i].astype(F32)).astype(BF16)

    def later_hop(k):
        count = quarter >> (k - 1)
        return remote(
            G.at[0, piece(away[k], count)], R2.at[k - 1, pl.ds(0, count)], r2_s.at[k - 1], r2_r.at[k - 1], peer[k]
        )

    def fold_later(k):
        count = quarter >> (k - 1)
        later_hop(k).wait_recv()
        rows = piece(keep[k], count)
        G[0, rows] = (G[0, rows].astype(F32) + R2[k - 1, pl.ds(0, count)].astype(F32)).astype(BF16)

    keep, away = {1: offs[3]}, {1: offs[2]}
    for k in range(2, levels):
        count = quarter >> (k - 1)
        keep[k] = keep[k - 1] + value[k] * count
        away[k] = keep[k - 1] + (1 - value[k]) * count
    least = quarter >> (levels - 2)

    def spread(src, offset, count, i, device):
        return remote(src, gw_hbm.at[core, piece(offset, count)], ag_s.at[i], ag_r.at[i], device)

    def final_at(offset, count):
        return gw_hbm.at[core, piece(offset, count)]

    own_out = pltpu.make_async_copy(G.at[0, piece(keep[levels - 1], least)], final_at(keep[levels - 1], least), s_out.at[2])

    def wider(k):
        count = quarter >> (k - 1)
        return spread(final_at(keep[k], count), keep[k], count, 7 + k, peer[k])

    def chip_copy(i):
        src = source if i == 3 else final_at(offs[i], quarter)
        return remote(src, final_at(offs[i], quarter), oc_s.at[i], oc_r.at[i], twin)

    source = final_at(offs[3], quarter) if levels > 2 else G.at[0, piece(offs[3], quarter)]
    third = quarter // 3

    def own_to(k, i):
        src = source.at[pl.ds(i * third, third)]
        return spread(src, offs[3] + i * third, third, (1 - k) * 3 + i, peer[k])

    def pass_on(i):
        begin = offs[2] + i * third
        return spread(final_at(begin, third), begin, third, 6 + i, peer[0])

    def last_out(i):
        begin = offs[0] + i * third
        return remote(final_at(begin, third), final_at(begin, third), lo_s.at[i], lo_r.at[i], twin)

    def small_hop(k):
        return remote(sms.at[k], smr.at[k], sm_s.at[k], sm_r.at[k], twin if k == 0 else peer[k - 1])

    def small_begin(k):
        sms[k] = smv[...]
        small_hop(k).start()

    def small_end(k):
        small_hop(k).wait_recv()
        smv[...] += smr[k]

    def small_sum(begin=0):
        for k in range(begin, levels + 1):
            small_begin(k)
            small_end(k)

    def sum_first():
        def small(*calls):
            @pl.when(section == 0)
            def _():
                for call, k in calls:
                    call(k)

        small((small_begin, 0))
        fold_first(0)
        later_hop(1).start()
        small((small_end, 0))
        fold_first(1)
        small((small_begin, 1), (small_end, 1), (small_begin, 2))
        fold_later(1)
        small((small_end, 2))
        for k in range(2, levels):
            later_hop(k).start()
            fold_later(k)
        own_out.start()
        if levels > 2:
            own_out.wait()
            for k in range(levels - 1, 1, -1):
                wider(k).start()
                wider(k).wait_recv()

        pl.when(section == 0)(lambda: small_sum(3))
        pl.when(section > 0)(lambda: small_sum(4))
        for i in range(3):
            own_to(1, i).start()
            own_to(0, i).start()
        chip_copy(3).start()

    def sum_next():
        for i in range(3):
            own_to(1, i).wait_recv()
            pass_on(i).start()
        chip_copy(2).start()


    def step(i, carry):
        forward = jnp.where(first_layer, i < n_rows, lax.rem(i, 2) == 0) & (i < 2 * n_rows)
        backward = jnp.where(first_layer, i >= n_rows, lax.rem(i, 2) == 1) & (i < 2 * n_rows)
        r = jnp.where(first_layer, lax.rem(i, n_rows), lax.rem(i // 2, n_rows))
        last = i == 2 * n_rows

        pl.when(forward)(lambda: row_forward(r))
        pl.when((section == 0) & (i == n_rows - 1))(take_turns)
        pl.when(backward)(lambda: row_backward(r))

        @pl.when(last)
        def _():
            store_ready()

            @pl.when(parity == 1)
            def _():
                smv[0:2] = smv[4:6]

            grads()

        late = first_layer & last
        pl.when((backward & jnp.logical_not(first_layer & (r == n_rows - 1))) | late)(
            lambda: part_back(jnp.where(late, n_rows - 1, r))
        )

        now = jnp.where(late, n_rows - 1, r)
        in_turn = backward & jnp.logical_not(first_layer & (r == n_rows - 1))
        pl.when(((section == 2) & in_turn) | ((section == 0) & (in_turn | late)))(lambda: mix_backward(now, gout))
        return carry

    lax.fori_loop(0, 2 * n_rows + 1, step, 0)

    @pl.when(section == 0)
    def _():
        store_ig(gmix).start()

    sum_first()
    sum_next()

    @pl.when(section == 1)
    def _():
        for r in range(n_rows):
            join_parts(r, gmix)
        store_ig(gmix).start()

    small_ref[...] = smv[...]
    small_ref[3:4, 0 : width // 2] = smv[3:4, pl.ds(pl.multiple_of(parity * (width // 2), 128), width // 2)]

    for i in range(3):
        own_to(0, i).wait_recv()
    chip_copy(1).start()
    for i in range(3):
        pass_on(i).wait_recv()
        last_out(i).start()
    for i in range(1, 4):
        chip_copy(i).wait_recv()
    for i in range(3):
        last_out(i).wait_recv()

    for copy in [chip_copy(3), chip_copy(2), chip_copy(1), first_hop(0), first_hop(1)]:
        copy.wait_send()
    for k in range(1, levels):
        later_hop(k).wait_send()
        if k > 1:
            wider(k).wait_send()
    for i in range(3):
        for copy in (own_to(1, i), own_to(0, i), pass_on(i), last_out(i)):
            copy.wait_send()
    for k in range(levels + 1):
        small_hop(k).wait_send()
    for i in range(4):
        to_twin(i, place_twin(i)).wait_send()
    if levels == 2:
        own_out.wait()
    store_so(h1).wait()
    store_ig(gout).wait()

    def sent(*makers):
        for r in range(n_rows):
            for t in range(chunks):
                for make in makers:
                    make(r, t).wait_send()

    pl.when(section == 0)(lambda: sent(lambda r, t: send_pb(r, t, rxa)))

    @pl.when(section == 0)
    def _():
        for r in range(n_rows):
            for t in range(chunks // 2, chunks):
                send_pa(r, t).wait_send()

    pl.when(section == 1)(lambda: sent(lambda r, t: send_h(r, t, hout, up), lambda r, t: send_g(r, t, dzb, down)))

    @pl.when(section == 2)
    def _():
        sent(lambda r, t: send_h(r, t, hin, up), lambda r, t: send_g(r, t, gmix, down))

    weights_sent()


def widen(
    so_in, ig_in, gw_in, small, so, ig, gain, bias, w_in, b_in, w_out, b_out, so_b, ig_b, gw_b, ig_f, w1_f, w2_f, s_in, s_out
):
    n_rows = ig_b.shape[0]
    width, half = w1_f.shape
    part = half // 4
    loads = []
    for i in range(8):
        rows = pl.ds((i // 2) * part, part)
        loads.append(pltpu.make_async_copy(gw_in.at[i % 2, rows], gw_b.at[i % 2, rows], s_in.at[i]))
    for r in range(n_rows):
        loads.append(pltpu.make_async_copy(ig_in.at[r], ig_b.at[r], s_in.at[9 + r]))
    loads.append(pltpu.make_async_copy(so_in, so_b, s_in.at[8]))
    for load in loads:
        load.start()
    width_half = width // 2
    gain[...] = small[0:1, 0:width]
    bias[...] = small[1:2, 0:width]
    b_in[...] = small[2:3, :]
    b_out[...] = small[3:4, 0:width_half]
    stores = []
    for i in range(4):
        rows = pl.ds(i * part, part)
        loads[2 * i].wait()
        w1_f[:, rows] = gw_b[0, rows].T.astype(F32)
        stores.append(pltpu.make_async_copy(w1_f.at[:, rows], w_in.at[0, :, rows], s_out.at[1 + 2 * i]))
        stores[-1].start()
        loads[2 * i + 1].wait()
        w2_f[rows] = gw_b[1, rows].astype(F32)
        stores.append(pltpu.make_async_copy(w2_f.at[rows], w_out.at[0, rows], s_out.at[2 + 2 * i]))
        stores[-1].start()
    for r in range(n_rows):
        loads[8 + r].wait()
        ig_f[r] = ig_b[r].astype(F32)
        stores.append(pltpu.make_async_copy(ig_f.at[r], ig.at[0, r], s_out.at[9 + r]))
        stores[-1].start()
    loads[-1].wait()
    stores.append(pltpu.make_async_copy(so_b, so.at[0], s_out.at[0]))
    stores[-1].start()
    for store in stores:
        store.wait()


def per_device(block_input, out_cotangent, lengths, ln_gain, ln_bias, w_in, b_in, w_out, b_out):
    n_rows, seq, width = block_input.shape
    half = w_in.shape[2]
    dp_count = lax.axis_size("dp")
    levels = int(math.log2(dp_count)) - 1
    chunks = seq // CHUNK
    quarter = half // 4
    cos_w, sin_w = dft_pair(width)
    cos_s, sin_s = dft_pair(seq)
    wt = jnp.asarray(np.concatenate([cos_w, sin_w], axis=1).astype(ml_dtypes.bfloat16))
    st = jnp.asarray(np.concatenate([cos_s, -sin_s], axis=1).astype(ml_dtypes.bfloat16))
    row_block = (n_rows, seq, width)
    dma = pltpu.SemaphoreType.DMA
    vmem = pl.BlockSpec(memory_space=pltpu.VMEM)
    anywhere = pl.BlockSpec(memory_space=pl.ANY)
    by_chunk = [dma((n_rows, chunks))] * 8
    scratch = [
        pltpu.VMEM((width, half), BF16),
        pltpu.VMEM((half, width), BF16),
        pltpu.VMEM((width, half), BF16),
        pltpu.VMEM((half, width), BF16),
        pltpu.VMEM((width, 2 * width), BF16),
        pltpu.VMEM((seq, 2 * seq), BF16),
        *[pltpu.VMEM(row_block, BF16) for _ in range(9)],
        pltpu.VMEM((n_rows, seq, half), BF16),
        pltpu.VMEM((n_rows, seq, half), BF16),
        pltpu.VMEM((1, seq, half), BF16),
        pltpu.VMEM((n_rows, seq, half), BF16),
        pltpu.VMEM((seq, 2 * width), BF16),
        pltpu.VMEM((seq, width), BF16),
        pltpu.VMEM(row_block, F32),
        pltpu.VMEM(row_block, F32),
        pltpu.VMEM((n_rows, seq, 1), F32),
        pltpu.VMEM((n_rows, seq, 1), F32),
        pltpu.VMEM((2, 8, half), F32),
        pltpu.VMEM((2, half, width), BF16),
        pltpu.VMEM((half, width), BF16),
        pltpu.VMEM((2, quarter, width), BF16),
        pltpu.VMEM((levels - 1, quarter, width), BF16),
        pltpu.VMEM((levels + 1, 8, half), F32),
        pltpu.VMEM((levels + 1, 8, half), F32),
        pltpu.VMEM((8, half), F32),
        pltpu.SemaphoreType.REGULAR,
        dma((6,)),
        dma((3,)),
        dma,
        dma,
        *by_chunk,
        *[dma((4,))] * 6,
        dma((4,)),
        dma((4,)),
        dma((4,)),
        dma((4,)),
        dma((2,)),
        dma((2,)),
        dma((levels - 1,)),
        dma((levels - 1,)),
        dma((7 + levels,)),
        dma((7 + levels,)),
        dma((4,)),
        dma((4,)),
        dma((3,)),
        dma((3,)),
        dma((levels + 1,)),
        dma((levels + 1,)),
    ]
    section_out, input_grad, weight_grad, small = pl.pallas_call(
        functools.partial(relay, dp_count),
        out_shape=(
            jax.ShapeDtypeStruct(row_block, BF16),
            jax.ShapeDtypeStruct(row_block, BF16),
            jax.ShapeDtypeStruct((2, half, width), BF16),
            jax.ShapeDtypeStruct((8, half), F32),
        ),
        in_specs=[
            pl.BlockSpec(memory_space=pltpu.SMEM),
            anywhere,
            anywhere,
            vmem,
            vmem,
            vmem,
            vmem,
            anywhere,
            anywhere,
            anywhere,
            anywhere,
        ],
        out_specs=(anywhere, anywhere, anywhere, vmem),
        scratch_shapes=scratch,
        compiler_params=pltpu.CompilerParams(
            collective_id=0, has_side_effects=True, vmem_limit_bytes=62 * 2**20
        ),
        name="fnet_relay",
    )(lengths, block_input, out_cotangent, ln_gain, ln_bias, b_in, b_out, w_in[0], w_out[0], wt, st)
    return pl.pallas_call(
        widen,
        out_shape=(
            jax.ShapeDtypeStruct((1, *row_block), BF16),
            jax.ShapeDtypeStruct((1, *row_block), F32),
            jax.ShapeDtypeStruct((1, width), F32),
            jax.ShapeDtypeStruct((1, width), F32),
            jax.ShapeDtypeStruct((1, width, half), F32),
            jax.ShapeDtypeStruct((1, half), F32),
            jax.ShapeDtypeStruct((1, half, width), F32),
            jax.ShapeDtypeStruct((1, width // 2), F32),
        ),
        in_specs=[anywhere, anywhere, anywhere, vmem],
        out_specs=(anywhere, anywhere, vmem, vmem, anywhere, vmem, anywhere, vmem),
        scratch_shapes=[
            pltpu.VMEM(row_block, BF16),
            pltpu.VMEM(row_block, BF16),
            pltpu.VMEM((2, half, width), BF16),
            pltpu.VMEM(row_block, F32),
            pltpu.VMEM((width, half), F32),
            pltpu.VMEM((half, width), F32),
            dma((9 + n_rows,)),
            dma((9 + n_rows,)),
        ],
        compiler_params=pltpu.CompilerParams(vmem_limit_bytes=62 * 2**20),
        name="widen",
    )(section_out, input_grad, weight_grad, small)


def solution(mesh):
    in_specs = (
        P("dp", None, None),
        P("dp", None, None),
        P("dp"),
        P("section", None),
        P("section", None),
        P("section", None, None),
        P("section", None),
        P("section", None, None),
        P("section", None),
    )
    out_specs = (
        P("section", "dp", None, None),
        P("section", "dp", None, None),
        P("section", None),
        P("section", None),
        P("section", None, None),
        P("section", None),
        P("section", None, None),
        P("section", None),
    )
    return jax.shard_map(
        per_device, mesh=mesh, in_specs=in_specs, out_specs=out_specs, check_vma=False
    )
```

```python
import functools
import math

import jax
import jax.numpy as jnp
import ml_dtypes
import numpy as np
from jax import lax
from jax.experimental import pallas as pl
from jax.experimental.pallas import tpu as pltpu
from jax.sharding import PartitionSpec as P

MESH = pl.DeviceIdType.MESH
F32, BF16 = jnp.float32, jnp.bfloat16
EPS = 1e-05
CHUNK = 128
WIDE = 2
ROOT_HALF = 1.0 / math.sqrt(2.0)
PDF_SCALE = 1.0 / math.sqrt(2.0 * math.pi)


def dft_pair(length):
    positions = np.arange(length, dtype=np.int64)
    angle = (positions[:, None] * positions[None, :] % length) * (2.0 * math.pi / length)
    scale = 1.0 / math.sqrt(length)
    return np.cos(angle) * scale, np.sin(angle) * scale


def dot(a, b):
    return jnp.dot(a, b, preferred_element_type=F32)


def dot_cols(a, b):
    return lax.dot_general(a, b, (((1,), (1,)), ((), ())), preferred_element_type=F32)


def dot_rows(a, b):
    return lax.dot_general(a, b, (((0,), (0,)), ((), ())), preferred_element_type=F32)


def gelu_pair(v):
    cdf = 0.5 * (1.0 + lax.erf(v * ROOT_HALF))
    return v * cdf, cdf + v * (jnp.exp(-0.5 * v * v) * PDF_SCALE)


def normalize(z):
    centre = z - jnp.mean(z, axis=-1, keepdims=True)
    spread = jnp.mean(centre * centre, axis=-1, keepdims=True)
    inverse = lax.rsqrt(spread + EPS)
    return centre * inverse, inverse


def norm_back(dy, normed, inverse, gain):
    e = dy * gain
    return inverse * (
        e - jnp.mean(e, axis=-1, keepdims=True) - normed * jnp.mean(e * normed, axis=-1, keepdims=True)
    )


def remote(src, dst, send, recv, device):
    return pltpu.make_async_remote_copy(
        src_ref=src, dst_ref=dst, send_sem=send, recv_sem=recv, device_id=device, device_id_type=MESH
    )


def relay(
    dp_count,
    lengths, x_hbm, cot_hbm, gain_ref, bias_ref, b_in_ref, b_out_ref, w1_hbm, w2_hbm, wt_hbm, st_hbm,
    so_hbm, ig_hbm, gw_hbm, small_ref,
    w1, w2, w1x, w2x, wt, st, hin, gin, rxa, rxb, h1, hout, dzb, gout, gmix, act, gp, actx, gpx, sp, dm,
    zacc, nrm, inv, msk, par, G, RC, R1, R2, sms, smr, smv,
    turn, s_load, s_out, par_s, par_r, h_s, h_r, g_s, g_r, pa_s, pa_r, pb_s, pb_r,
    wz_s, wz_r, wa_s, wa_r, wb_s, wb_r, wc_s, wc_r, rc_s, rc_r, r1_s, r1_r, r2_s, r2_r, ag_s, ag_r, oc_s, oc_r, lo_s, lo_r, sm_s, sm_r,
):
    section = lax.axis_index("section")
    d = lax.axis_index("dp")
    core = lax.rem(d, 2)
    parity = lax.rem(section, 2)
    n_rows, seq, width = hin.shape
    half = w1.shape[1]
    chunks = seq // CHUNK
    tiles = half // 512
    levels = int(math.log2(dp_count)) - 1
    bits = [2 << k for k in range(levels)]

    def flipped(bit):
        return d + bit - 2 * bit * lax.rem(d // bit, 2)

    def by_core(first, second):
        return first + core * (second - first)

    bit_value = [lax.rem(d // b, 2) for b in bits]
    value = [by_core(bit_value[k], bit_value[levels - 1 - k]) for k in range(levels)]
    peer = [(section, by_core(flipped(bits[k]), flipped(bits[levels - 1 - k]))) for k in range(levels)]
    twin = (section, d + 1 - 2 * core)
    pair = (section + 1 - 2 * parity, d)
    up = (section + 1, d)
    down = (section - 1, d)

    def rows_of(t):
        return pl.ds(t * CHUNK, CHUNK)

    wide_rows = [pl.ds(i * WIDE * CHUNK, WIDE * CHUNK) for i in range(chunks // WIDE)]

    barrier = pltpu.get_barrier_semaphore()

    def greet(device):
        pl.semaphore_signal(barrier, inc=1, device_id=device, device_id_type=MESH)

    greet(twin)
    for k in range(levels):
        greet(peer[k])
    pl.when(section > 0)(lambda: greet(down))
    pl.when(section < 3)(lambda: greet(up))

    load_x = pltpu.make_async_copy(x_hbm, hin, s_load.at[0])
    load_cot = pltpu.make_async_copy(cot_hbm, gin, s_load.at[1])
    load_wt = pltpu.make_async_copy(wt_hbm, wt, s_load.at[2])
    load_st = pltpu.make_async_copy(st_hbm, st, s_load.at[3])
    load_w1 = pltpu.make_async_copy(w1_hbm, w1, s_load.at[4])
    load_w2 = pltpu.make_async_copy(w2_hbm, w2, s_load.at[5])

    @pl.when(section < 2)
    def _():
        load_x.start()
        load_wt.start()
        load_st.start()
        load_w1.start()
        load_w2.start()

    @pl.when(section >= 2)
    def _():
        load_w1.start()
        load_w2.start()
        load_wt.start()
        load_st.start()
        load_cot.start()

    par[parity] = jnp.zeros(par.shape[1:], F32)
    par[parity, 0:1, 0:width] = gain_ref[...]
    par[parity, 1:2, 0:width] = bias_ref[...]
    par[parity, 2:3, :] = b_in_ref[...].astype(F32)
    par[parity, 3:4, pl.ds(pl.multiple_of(parity * (width // 2), 128), width // 2)] = b_out_ref[...].astype(F32)
    smv[...] = jnp.zeros(smv.shape, F32)
    for r in range(n_rows):
        position = lax.broadcasted_iota(jnp.int32, (seq, 1), 0)
        msk[r] = jnp.where(position < lengths[r], 1.0, 0.0).astype(F32)

    pl.semaphore_wait(barrier, 1 + levels + jnp.where((section == 0) | (section == 3), 1, 2))

    swap_par = remote(par.at[parity], par.at[parity], par_s, par_r, pair)
    swap_par.start()

    quarter = half // 4
    chip = lax.rem(d // 2, 4)
    chip_far = 3 - chip
    chip_a = chip + 1 - 2 * lax.rem(chip, 2)
    chip_b = 3 - chip_a
    near_a = (section, flipped(2))
    near_b = (section, flipped(4))

    def swap(which, q, i, n, own, send, recv, device):
        if which == 0:
            from_ref, to_ref = (w1_hbm if own else w1x), w1x
        else:
            from_ref, to_ref = (w2_hbm if own else w2x), w2x
        third = to_ref.shape[0] // 12
        part = pl.ds(pl.multiple_of((3 * q + i) * third, 16), n * third)
        return remote(from_ref.at[part], to_ref.at[part], send, recv, device)

    def each_core(fn):
        for which in range(2):
            pl.when(core == which)(functools.partial(fn, which))

    def z_hop(which, i):
        if i < 3:
            return swap(which, chip, i, 1, True, wz_s.at[i], wz_r.at[i], pair)
        return swap(which, chip_far, 0, 1, True, wz_s.at[3], wz_r.at[3], pair)

    def a_hop(which, i):
        if i < 3:
            return swap(which, chip, i, 1, False, wa_s.at[i], wa_r.at[i], near_a)
        return swap(which, chip_b, 1, 1, False, wa_s.at[3], wa_r.at[3], near_a)

    def b_hop(which, i):
        if i < 3:
            return swap(which, chip, i, 1, False, wb_s.at[i], wb_r.at[i], near_b)
        return swap(which, chip_a, 2, 1, False, wb_s.at[3], wb_r.at[3], near_b)

    def a_got(which, i):
        if i < 3:
            return swap(which, chip_a, i, 1, False, wa_s.at[i], wa_r.at[i], near_a)
        return swap(which, chip_far, 1, 1, False, wa_s.at[3], wa_r.at[3], near_a)

    def b_got(which, i):
        if i < 3:
            return swap(which, chip_b, i, 1, False, wb_s.at[i], wb_r.at[i], near_b)
        return swap(which, chip_far, 2, 1, False, wb_s.at[3], wb_r.at[3], near_b)

    def twin_hop(which, i):
        q = (chip, chip_a, chip_b, chip_far)[i]
        return swap(which, q, 0, 3, False, wc_s.at[i], wc_r.at[i], twin)

    def weights_begin():
        def go(which):
            for i in range(4):
                z_hop(which, i).start()

        each_core(go)

    def weights_spread():
        def go(which):
            for i in range(3):
                z_hop(which, i).wait_recv()
                a_hop(which, i).start()
                b_hop(which, i).start()
            twin_hop(which, 0).start()
            b_got(which, 0).wait_recv()
            b_got(which, 1).wait_recv()
            a_hop(which, 3).start()
            for i in range(3):
                a_got(which, i).wait_recv()
            b_hop(which, 3).start()
            twin_hop(which, 1).start()

        each_core(go)

    def weights_end():
        def go(which):
            b_got(which, 2).wait_recv()
            twin_hop(which, 2).start()
            z_hop(which, 3).wait_recv()
            a_got(which, 3).wait_recv()
            b_got(which, 3).wait_recv()
            twin_hop(which, 3).start()

        each_core(go)

    def weights_ready():
        def go(which):
            for i in range(4):
                twin_hop(1 - which, i).wait_recv()

        each_core(go)

    def weights_sent():
        def go(which):
            for i in range(4):
                pl.when(section > 0)(z_hop(which, i).wait_send)

                @pl.when(section != 1)
                def _():
                    a_hop(which, i).wait_send()
                    b_hop(which, i).wait_send()
                    twin_hop(which, i).wait_send()

        each_core(go)

    def gain_of(sub):
        return par[sub, 0:1, 0:width]

    def bias_of(sub):
        return par[sub, 1:2, 0:width]

    def mix_forward(r):
        for j in range(2 * width // 512):
            cols = pl.ds(j * 512, 512)
            sp[:, cols] = dot(hin[r], wt[:, cols]).astype(BF16)
        pl.when(r == 0)(swap_par.wait)
        for t in range(chunks):
            rows = rows_of(t)
            z = (
                hin[r, rows].astype(F32)
                + dot(st[rows, 0:seq], sp[:, 0:width])
                + dot(st[rows, seq : 2 * seq], sp[:, width : 2 * width])
            )
            normed, inverse = normalize(z)
            nrm[r, rows] = normed
            inv[r, rows] = inverse
            h1[r, rows] = ((normed * gain_of(0) + bias_of(0)) * msk[r, rows]).astype(BF16)

    def inner(r, w_ref, b_row, act_ref, act_at, gp_ref):
        for j in range(tiles):
            cols = pl.ds(j * 512, 512)
            for t in range(chunks):
                rows = rows_of(t)
                pre = dot(h1[r, rows], w_ref[:, cols]) + b_row(cols)
                active, slope = gelu_pair(pre)
                act_ref[act_at, rows, cols] = active.astype(BF16)
                gp_ref[r, rows, cols] = slope.astype(BF16)

    def b_own(cols):
        return par[parity, 2:3, cols]

    def b_other(cols):
        return par[1 - parity, 2:3, cols]

    def outer_bias():
        return par[0, 3:4, 0:width] + par[1, 3:4, 0:width]

    def inner_back(r, w_ref, gp_ref, own):
        for j in range(tiles):
            cols = pl.ds(j * 512, 512)
            dactive = dot_cols(dzb[r], w_ref[cols, :]).astype(BF16).astype(F32)
            dpre = (dactive * gp_ref[r, :, cols].astype(F32)).astype(BF16)
            gp_ref[r, :, cols] = dpre
            if own:
                smv[2:3, cols] += jnp.sum(dpre.astype(F32), axis=0, keepdims=True)

    def ff_norm_back(r, rows, upstream, normed, inverse):
        dy = upstream.astype(F32) * msk[r, rows]
        smv[4:5, 0:width] += jnp.sum(dy * normed, axis=0, keepdims=True)
        smv[5:6, 0:width] += jnp.sum(dy, axis=0, keepdims=True)
        dz = norm_back(dy, normed, inverse, gain_of(1))
        zacc[r, rows] = dz
        rounded = dz.astype(BF16)
        dzb[r, rows] = rounded
        smv[3:4, 0:width] += jnp.sum(rounded.astype(F32), axis=0, keepdims=True)

    def mix_backward(r, upstream_ref):
        for t in range(chunks):
            rows = rows_of(t)
            normed = nrm[r, rows]
            dy = upstream_ref[r, rows].astype(F32) * msk[r, rows]
            smv[0:1, 0:width] += jnp.sum(dy * normed, axis=0, keepdims=True)
            smv[1:2, 0:width] += jnp.sum(dy, axis=0, keepdims=True)
            dz = norm_back(dy, normed, inv[r, rows], gain_of(0))
            zacc[r, rows] = dz
            dm[rows] = dz.astype(BF16)
        for j in range(2):
            part = dot(st[:, j * seq : (j + 1) * seq], dm[...])
            sp[:, j * width : (j + 1) * width] = part.astype(BF16)
        for t in range(chunks):
            rows = rows_of(t)
            grad = (
                zacc[r, rows]
                + dot(sp[rows, 0:width], wt[:, 0:width])
                + dot(sp[rows, width : 2 * width], wt[:, width : 2 * width])
            )
            gmix[r, rows] = grad.astype(BF16)
            pl.when(section == 2)(send_g(r, t, gmix, down).start)

    def send_h(r, t, src, to):
        return remote(src.at[r, rows_of(t)], hin.at[r, rows_of(t)], h_s.at[r, t], h_r.at[r, t], to)

    def send_g(r, t, src, to):
        return remote(src.at[r, rows_of(t)], gin.at[r, rows_of(t)], g_s.at[r, t], g_r.at[r, t], to)

    def send_pa(r, t):
        return remote(hout.at[r, rows_of(t)], rxa.at[r, rows_of(t)], pa_s.at[r, t], pa_r.at[r, t], pair)

    def send_pb(r, t, src):
        return remote(src.at[r, rows_of(t)], rxb.at[r, rows_of(t)], pb_s.at[r, t], pb_r.at[r, t], pair)

    first_layer = section < 2
    whole = section != 1

    def finish_with_pair(r):
        for t in range(chunks):
            rows = rows_of(t)
            send_pa(r, t).wait_recv()
            normed, inverse = normalize(zacc[r, rows] + rxa[r, rows].astype(F32))
            nrm[r, rows] = normed
            inv[r, rows] = inverse
            hout[r, rows] = ((normed * gain_of(1) + bias_of(1)) * msk[r, rows]).astype(BF16)
            send_h(r, t, hout, up).start()

    def row_forward(r):
        @pl.when(first_layer)
        def _():
            hin[r] = (hin[r].astype(F32) * msk[r]).astype(BF16)

        @pl.when(jnp.logical_not(first_layer))
        def _():
            for t in range(chunks):
                send_h(r, t, hin, up).wait_recv()
                pl.when(section == 2)(send_h(r, t, hin, up).start)

        mix_forward(r)
        inner(r, w1, b_own, act, r, gp)

        @pl.when(first_layer)
        def _():
            for t in range(chunks):
                rows = rows_of(t)
                part = dot(act[r, rows], w2[...])

                @pl.when(section == 0)
                def _():
                    hout[r, rows] = part.astype(BF16)
                    pl.when((core == 0) & (r == 0))(send_pa(r, t).start)

                @pl.when(section == 1)
                def _():
                    zacc[r, rows] = h1[r, rows].astype(F32) + part + outer_bias()

        pl.when(section == 1)(lambda: finish_with_pair(r))

    def send_row(r):
        for t in range(chunks):
            send_pa(r, t).start()

    def half_sent(r):
        for t in range(chunks // 2):
            send_pa(r, t).wait_send()

    def hand_over(r):
        half_sent(r)
        pl.semaphore_signal(turn, inc=1, device_id=twin, device_id_type=MESH)

    def take_turns():
        @pl.when(core == 0)
        def _():
            hand_over(0)
            for r in range(1, n_rows):
                pl.semaphore_wait(turn, 1)
                send_row(r)
                hand_over(r)

        @pl.when(core == 1)
        def _():
            for r in range(n_rows):
                pl.semaphore_wait(turn, 1)
                send_row(r)
                (hand_over if r < n_rows - 1 else half_sent)(r)

    def part_back(r):
        for i, rows in enumerate(wide_rows):
            part = dot_cols(gp[r, rows], w1[...])

            @pl.when(section == 0)
            def _():
                zacc[r, rows] = dzb[r, rows].astype(F32)
                rxa[r, rows] = part.astype(BF16)
                for t in range(i * WIDE, (i + 1) * WIDE):
                    send_pb(r, t, rxa).start()

            zacc[r, rows] += part

            @pl.when(whole)
            def _():
                gout[r, rows] = (zacc[r, rows] + dot_cols(gpx[r, rows], w1x[...])).astype(BF16)

    def row_backward(r):
        pl.when((section == 0) & (r == 0))(weights_spread)
        pl.when(((section == 0) | ((section > 1) & (core == 0))) & (r == 0))(weights_end)
        pl.when(whole & (r == 0))(weights_ready)
        pl.when(whole)(lambda: inner(r, w1x, b_other, actx, 0, gpx))

        @pl.when(section == 0)
        def _():
            for t in range(chunks):
                rows = rows_of(t)
                send_g(r, t, dzb, up).wait_recv()
                dzb[r, rows] = gin[r, rows]
                smv[3:4, 0:width] += jnp.sum(gin[r, rows].astype(F32), axis=0, keepdims=True)

        @pl.when(section == 1)
        def _():
            for t in range(chunks):
                rows = rows_of(t)
                send_g(r, t, dzb, down).wait_recv()
                ff_norm_back(r, rows, gin[r, rows], nrm[r, rows], inv[r, rows])
                send_g(r, t, dzb, down).start()

        @pl.when(jnp.logical_not(first_layer))
        def _():
            for t in range(chunks):
                rows = rows_of(t)
                z = (
                    h1[r, rows].astype(F32)
                    + dot(act[r, rows], w2[...])
                    + dot(actx[0, rows], w2x[...])
                    + outer_bias()
                )
                normed, inverse = normalize(z)
                hout[r, rows] = ((normed * gain_of(1) + bias_of(1)) * msk[r, rows]).astype(BF16)
                ff_norm_back(r, rows, gin[r, rows], normed, inverse)

        inner_back(r, w2, gp, True)

        pl.when(whole)(lambda: inner_back(r, w2x, gpx, False))

    def join_parts(r, to):
        for t in range(chunks):
            rows = rows_of(t)
            send_pb(r, t, rxa).wait_recv()
            to[r, rows] = (zacc[r, rows] + rxb[r, rows].astype(F32)).astype(BF16)

    pl.when(section > 0)(weights_begin)
    load_wt.wait()
    load_st.wait()
    load_w1.wait()
    load_w2.wait()

    @pl.when(first_layer)
    def _():
        load_x.wait()

    @pl.when(jnp.logical_not(first_layer))
    def _():
        load_cot.wait()
        weights_spread()
        pl.when(core == 1)(weights_end)

    def store_so(src):
        return pltpu.make_async_copy(src, so_hbm, s_out.at[0])

    def store_ig(src):
        return pltpu.make_async_copy(src, ig_hbm, s_out.at[1])

    def store_ready():
        pl.when(parity == 0)(lambda: store_so(h1).start())
        pl.when(parity == 1)(lambda: store_so(hout).start())
        pl.when(section == 2)(lambda: store_ig(gmix).start())
        pl.when(section == 3)(lambda: store_ig(gout).start())

    def place(a, b, i):
        first, second = i // 2, lax.rem(i, 2)
        return ((1 - a + first * (2 * a - 1)) * 2 + 1 - b + second * (2 * b - 1)) * quarter

    def place_1(i):
        return place(bit_value[0], bit_value[1], i)

    def place_2(i):
        return place(bit_value[levels - 1], bit_value[levels - 2], i)

    def place_own(i):
        return by_core(place_1(i), place_2(i))

    def place_twin(i):
        return by_core(place_2(i), place_1(i))

    offs = [place_own(i) for i in range(4)]

    def piece(offset, count):
        return pl.ds(pl.multiple_of(offset, 16), count)

    def lanes(offset):
        return pl.ds(pl.multiple_of(offset, 128), quarter)

    def to_twin(i, offset):
        return remote(G.at[1, piece(offset, quarter)], RC.at[piece(offset, quarter)], rc_s.at[i], rc_r.at[i], twin)

    def first_hop(i):
        return remote(G.at[0, piece(place_own(i), quarter)], R1.at[i], r1_s.at[i], r1_r.at[i], peer[0])

    def fold_twin(i):
        to_twin(i, place_own(i)).wait_recv()
        rows = piece(place_own(i), quarter)
        G[0, rows] = (G[0, rows].astype(F32) + RC[rows].astype(F32)).astype(BF16)

    def grads_quarter(i):
        at_1, at_2 = place_1(i), place_2(i)
        grad_1 = dot_rows(gp[0, :, lanes(at_1)], h1[0])
        grad_2 = dot_rows(act[0, :, lanes(at_2)], dzb[0])
        for r in range(1, n_rows):
            grad_1 += dot_rows(gp[r, :, lanes(at_1)], h1[r])
            grad_2 += dot_rows(act[r, :, lanes(at_2)], dzb[r])
        G[core, piece(at_1, quarter)] = grad_1.astype(BF16)
        G[1 - core, piece(at_2, quarter)] = grad_2.astype(BF16)
        to_twin(i, place_twin(i)).start()

    def grads():
        for i in range(4):
            pl.when(section > 0)(lambda: small_begin(i) if i <= levels else None)
            grads_quarter(i)
            if i > 0:
                fold_twin(i - 1)
            if 1 <= i < 3:
                first_hop(i - 1).start()
            pl.when(section > 0)(lambda: small_end(i) if i <= levels else None)
        fold_twin(3)

    def fold_first(i):
        first_hop(i).wait_recv()
        rows = piece(offs[2 + i], quarter)
        G[0, rows] = (G[0, rows].astype(F32) + R1[i].astype(F32)).astype(BF16)

    def later_hop(k):
        count = quarter >> (k - 1)
        return remote(
            G.at[0, piece(away[k], count)], R2.at[k - 1, pl.ds(0, count)], r2_s.at[k - 1], r2_r.at[k - 1], peer[k]
        )

    def fold_later(k):
        count = quarter >> (k - 1)
        later_hop(k).wait_recv()
        rows = piece(keep[k], count)
        G[0, rows] = (G[0, rows].astype(F32) + R2[k - 1, pl.ds(0, count)].astype(F32)).astype(BF16)

    keep, away = {1: offs[3]}, {1: offs[2]}
    for k in range(2, levels):
        count = quarter >> (k - 1)
        keep[k] = keep[k - 1] + value[k] * count
        away[k] = keep[k - 1] + (1 - value[k]) * count
    least = quarter >> (levels - 2)

    def spread(src, offset, count, i, device):
        return remote(src, gw_hbm.at[core, piece(offset, count)], ag_s.at[i], ag_r.at[i], device)

    def final_at(offset, count):
        return gw_hbm.at[core, piece(offset, count)]

    own_out = pltpu.make_async_copy(G.at[0, piece(keep[levels - 1], least)], final_at(keep[levels - 1], least), s_out.at[2])

    def wider(k):
        count = quarter >> (k - 1)
        return spread(final_at(keep[k], count), keep[k], count, 7 + k, peer[k])

    def chip_copy(i):
        src = source if i == 3 else final_at(offs[i], quarter)
        return remote(src, final_at(offs[i], quarter), oc_s.at[i], oc_r.at[i], twin)

    source = final_at(offs[3], quarter) if levels > 2 else G.at[0, piece(offs[3], quarter)]
    third = quarter // 3

    def own_to(k, i):
        src = source.at[pl.ds(i * third, third)]
        return spread(src, offs[3] + i * third, third, (1 - k) * 3 + i, peer[k])

    def pass_on(i):
        begin = offs[2] + i * third
        return spread(final_at(begin, third), begin, third, 6 + i, peer[0])

    def last_out(i):
        begin = offs[0] + i * third
        return remote(final_at(begin, third), final_at(begin, third), lo_s.at[i], lo_r.at[i], twin)

    def small_hop(k):
        return remote(sms.at[k], smr.at[k], sm_s.at[k], sm_r.at[k], twin if k == 0 else peer[k - 1])

    def small_begin(k):
        sms[k] = smv[...]
        small_hop(k).start()

    def small_end(k):
        small_hop(k).wait_recv()
        smv[...] += smr[k]

    def small_sum(begin=0):
        for k in range(begin, levels + 1):
            small_begin(k)
            small_end(k)

    def sum_first():
        def small(*calls):
            @pl.when(section == 0)
            def _():
                for call, k in calls:
                    call(k)

        small((small_begin, 0))
        fold_first(0)
        later_hop(1).start()
        small((small_end, 0))
        fold_first(1)
        small((small_begin, 1), (small_end, 1), (small_begin, 2))
        fold_later(1)
        small((small_end, 2))
        for k in range(2, levels):
            later_hop(k).start()
            fold_later(k)
        own_out.start()
        if levels > 2:
            own_out.wait()
            for k in range(levels - 1, 1, -1):
                wider(k).start()
                wider(k).wait_recv()

        pl.when(section == 0)(lambda: small_sum(3))
        pl.when(section > 0)(lambda: small_sum(4))
        for i in range(3):
            own_to(1, i).start()
            own_to(0, i).start()
        chip_copy(3).start()

    def sum_next():
        for i in range(3):
            own_to(1, i).wait_recv()
            pass_on(i).start()
        chip_copy(2).start()


    def step(i, carry):
        forward = jnp.where(first_layer, i < n_rows, lax.rem(i, 2) == 0) & (i < 2 * n_rows)
        backward = jnp.where(first_layer, i >= n_rows, lax.rem(i, 2) == 1) & (i < 2 * n_rows)
        r = jnp.where(first_layer, lax.rem(i, n_rows), lax.rem(i // 2, n_rows))
        last = i == 2 * n_rows

        pl.when(forward)(lambda: row_forward(r))
        pl.when((section == 0) & (i == n_rows - 1))(take_turns)
        pl.when(backward)(lambda: row_backward(r))

        @pl.when(last)
        def _():
            store_ready()

            @pl.when(parity == 1)
            def _():
                smv[0:2] = smv[4:6]

            grads()

        put_off = first_layer & (core == 1)
        late = put_off & last
        in_turn = backward & jnp.logical_not(put_off & (r == n_rows - 1))
        pl.when(in_turn | late)(
            lambda: part_back(jnp.where(late, n_rows - 1, r))
        )

        now = jnp.where(late, n_rows - 1, r)
        pl.when(((section == 2) & in_turn) | ((section == 0) & (in_turn | late)))(lambda: mix_backward(now, gout))
        return carry

    lax.fori_loop(0, 2 * n_rows + 1, step, 0)

    @pl.when(section == 0)
    def _():
        store_ig(gmix).start()

    sum_first()
    sum_next()

    @pl.when(section == 1)
    def _():
        for r in range(n_rows):
            join_parts(r, gmix)
        store_ig(gmix).start()

    small_ref[...] = smv[...]
    small_ref[3:4, 0 : width // 2] = smv[3:4, pl.ds(pl.multiple_of(parity * (width // 2), 128), width // 2)]

    for i in range(3):
        own_to(0, i).wait_recv()
    chip_copy(1).start()
    for i in range(3):
        pass_on(i).wait_recv()
        last_out(i).start()
    for i in range(1, 4):
        chip_copy(i).wait_recv()
    for i in range(3):
        last_out(i).wait_recv()

    for copy in [chip_copy(3), chip_copy(2), chip_copy(1), first_hop(0), first_hop(1)]:
        copy.wait_send()
    for k in range(1, levels):
        later_hop(k).wait_send()
        if k > 1:
            wider(k).wait_send()
    for i in range(3):
        for copy in (own_to(1, i), own_to(0, i), pass_on(i), last_out(i)):
            copy.wait_send()
    for k in range(levels + 1):
        small_hop(k).wait_send()
    for i in range(4):
        to_twin(i, place_twin(i)).wait_send()
    if levels == 2:
        own_out.wait()
    store_so(h1).wait()
    store_ig(gout).wait()

    def sent(*makers):
        for r in range(n_rows):
            for t in range(chunks):
                for make in makers:
                    make(r, t).wait_send()

    pl.when(section == 0)(lambda: sent(lambda r, t: send_pb(r, t, rxa)))

    @pl.when(section == 0)
    def _():
        for r in range(n_rows):
            for t in range(chunks // 2, chunks):
                send_pa(r, t).wait_send()

    pl.when(section == 1)(lambda: sent(lambda r, t: send_h(r, t, hout, up), lambda r, t: send_g(r, t, dzb, down)))

    @pl.when(section == 2)
    def _():
        sent(lambda r, t: send_h(r, t, hin, up), lambda r, t: send_g(r, t, gmix, down))

    weights_sent()


def widen(
    so_in, ig_in, gw_in, small, so, ig, gain, bias, w_in, b_in, w_out, b_out, so_b, ig_b, gw_b, ig_f, w1_f, w2_f, s_in, s_out
):
    n_rows = ig_b.shape[0]
    width, half = w1_f.shape
    part = half // 4
    loads = []
    for i in range(8):
        rows = pl.ds((i // 2) * part, part)
        loads.append(pltpu.make_async_copy(gw_in.at[i % 2, rows], gw_b.at[i % 2, rows], s_in.at[i]))
    for r in range(n_rows):
        loads.append(pltpu.make_async_copy(ig_in.at[r], ig_b.at[r], s_in.at[9 + r]))
    loads.append(pltpu.make_async_copy(so_in, so_b, s_in.at[8]))
    for load in loads:
        load.start()
    width_half = width // 2
    gain[...] = small[0:1, 0:width]
    bias[...] = small[1:2, 0:width]
    b_in[...] = small[2:3, :]
    b_out[...] = small[3:4, 0:width_half]
    stores = []
    for i in range(4):
        rows = pl.ds(i * part, part)
        loads[2 * i].wait()
        w1_f[:, rows] = gw_b[0, rows].T.astype(F32)
        stores.append(pltpu.make_async_copy(w1_f.at[:, rows], w_in.at[0, :, rows], s_out.at[1 + 2 * i]))
        stores[-1].start()
        loads[2 * i + 1].wait()
        w2_f[rows] = gw_b[1, rows].astype(F32)
        stores.append(pltpu.make_async_copy(w2_f.at[rows], w_out.at[0, rows], s_out.at[2 + 2 * i]))
        stores[-1].start()
    for r in range(n_rows):
        loads[8 + r].wait()
        ig_f[r] = ig_b[r].astype(F32)
        stores.append(pltpu.make_async_copy(ig_f.at[r], ig.at[0, r], s_out.at[9 + r]))
        stores[-1].start()
    loads[-1].wait()
    stores.append(pltpu.make_async_copy(so_b, so.at[0], s_out.at[0]))
    stores[-1].start()
    for store in stores:
        store.wait()


def per_device(block_input, out_cotangent, lengths, ln_gain, ln_bias, w_in, b_in, w_out, b_out):
    n_rows, seq, width = block_input.shape
    half = w_in.shape[2]
    dp_count = lax.axis_size("dp")
    levels = int(math.log2(dp_count)) - 1
    chunks = seq // CHUNK
    quarter = half // 4
    cos_w, sin_w = dft_pair(width)
    cos_s, sin_s = dft_pair(seq)
    wt = jnp.asarray(np.concatenate([cos_w, sin_w], axis=1).astype(ml_dtypes.bfloat16))
    st = jnp.asarray(np.concatenate([cos_s, -sin_s], axis=1).astype(ml_dtypes.bfloat16))
    row_block = (n_rows, seq, width)
    dma = pltpu.SemaphoreType.DMA
    vmem = pl.BlockSpec(memory_space=pltpu.VMEM)
    anywhere = pl.BlockSpec(memory_space=pl.ANY)
    by_chunk = [dma((n_rows, chunks))] * 8
    scratch = [
        pltpu.VMEM((width, half), BF16),
        pltpu.VMEM((half, width), BF16),
        pltpu.VMEM((width, half), BF16),
        pltpu.VMEM((half, width), BF16),
        pltpu.VMEM((width, 2 * width), BF16),
        pltpu.VMEM((seq, 2 * seq), BF16),
        *[pltpu.VMEM(row_block, BF16) for _ in range(9)],
        pltpu.VMEM((n_rows, seq, half), BF16),
        pltpu.VMEM((n_rows, seq, half), BF16),
        pltpu.VMEM((1, seq, half), BF16),
        pltpu.VMEM((n_rows, seq, half), BF16),
        pltpu.VMEM((seq, 2 * width), BF16),
        pltpu.VMEM((seq, width), BF16),
        pltpu.VMEM(row_block, F32),
        pltpu.VMEM(row_block, F32),
        pltpu.VMEM((n_rows, seq, 1), F32),
        pltpu.VMEM((n_rows, seq, 1), F32),
        pltpu.VMEM((2, 8, half), F32),
        pltpu.VMEM((2, half, width), BF16),
        pltpu.VMEM((half, width), BF16),
        pltpu.VMEM((2, quarter, width), BF16),
        pltpu.VMEM((levels - 1, quarter, width), BF16),
        pltpu.VMEM((levels + 1, 8, half), F32),
        pltpu.VMEM((levels + 1, 8, half), F32),
        pltpu.VMEM((8, half), F32),
        pltpu.SemaphoreType.REGULAR,
        dma((6,)),
        dma((3,)),
        dma,
        dma,
        *by_chunk,
        *[dma((4,))] * 6,
        dma((4,)),
        dma((4,)),
        dma((4,)),
        dma((4,)),
        dma((2,)),
        dma((2,)),
        dma((levels - 1,)),
        dma((levels - 1,)),
        dma((7 + levels,)),
        dma((7 + levels,)),
        dma((4,)),
        dma((4,)),
        dma((3,)),
        dma((3,)),
        dma((levels + 1,)),
        dma((levels + 1,)),
    ]
    section_out, input_grad, weight_grad, small = pl.pallas_call(
        functools.partial(relay, dp_count),
        out_shape=(
            jax.ShapeDtypeStruct(row_block, BF16),
            jax.ShapeDtypeStruct(row_block, BF16),
            jax.ShapeDtypeStruct((2, half, width), BF16),
            jax.ShapeDtypeStruct((8, half), F32),
        ),
        in_specs=[
            pl.BlockSpec(memory_space=pltpu.SMEM),
            anywhere,
            anywhere,
            vmem,
            vmem,
            vmem,
            vmem,
            anywhere,
            anywhere,
            anywhere,
            anywhere,
        ],
        out_specs=(anywhere, anywhere, anywhere, vmem),
        scratch_shapes=scratch,
        compiler_params=pltpu.CompilerParams(
            collective_id=0, has_side_effects=True, vmem_limit_bytes=62 * 2**20
        ),
        name="fnet_relay",
    )(lengths, block_input, out_cotangent, ln_gain, ln_bias, b_in, b_out, w_in[0], w_out[0], wt, st)
    return pl.pallas_call(
        widen,
        out_shape=(
            jax.ShapeDtypeStruct((1, *row_block), BF16),
            jax.ShapeDtypeStruct((1, *row_block), F32),
            jax.ShapeDtypeStruct((1, width), F32),
            jax.ShapeDtypeStruct((1, width), F32),
            jax.ShapeDtypeStruct((1, width, half), F32),
            jax.ShapeDtypeStruct((1, half), F32),
            jax.ShapeDtypeStruct((1, half, width), F32),
            jax.ShapeDtypeStruct((1, width // 2), F32),
        ),
        in_specs=[anywhere, anywhere, anywhere, vmem],
        out_specs=(anywhere, anywhere, vmem, vmem, anywhere, vmem, anywhere, vmem),
        scratch_shapes=[
            pltpu.VMEM(row_block, BF16),
            pltpu.VMEM(row_block, BF16),
            pltpu.VMEM((2, half, width), BF16),
            pltpu.VMEM(row_block, F32),
            pltpu.VMEM((width, half), F32),
            pltpu.VMEM((half, width), F32),
            dma((9 + n_rows,)),
            dma((9 + n_rows,)),
        ],
        compiler_params=pltpu.CompilerParams(vmem_limit_bytes=62 * 2**20),
        name="widen",
    )(section_out, input_grad, weight_grad, small)


def solution(mesh):
    in_specs = (
        P("dp", None, None),
        P("dp", None, None),
        P("dp"),
        P("section", None),
        P("section", None),
        P("section", None, None),
        P("section", None),
        P("section", None, None),
        P("section", None),
    )
    out_specs = (
        P("section", "dp", None, None),
        P("section", "dp", None, None),
        P("section", None),
        P("section", None),
        P("section", None, None),
        P("section", None),
        P("section", None, None),
        P("section", None),
    )
    return jax.shard_map(
        per_device, mesh=mesh, in_specs=in_specs, out_specs=out_specs, check_vma=False
    )
```
